512 devices in a mesh: row: 8 (over y), col: 4 (over x_lo, core), tm: 16 (over x_hi, z).
Axes of the slice: x: 4 (x_hi: 2, x_lo: 2; x = x_hi * 2 + x_lo), y: 8, z: 8, core: 2. Of those that a mesh axis runs over, the one named last changes fastest.
Arguments:
- filled_orbitals: bfloat16 [4, 1024, 1024], P('col', 'row', 'tm'), may hold values from -0.1875 to 0.1875
- empty_orbitals: bfloat16 [4, 1024, 3072], P('col', 'row', 'tm'), may hold values from -0.109375 to 0.109375
- filled_depth: bfloat16 [1024], P('tm'), may hold values from 0.019897461 to 2
- empty_depth: bfloat16 [3072], P('tm'), may hold values from 0.019897461 to 2
- time_points: float32 [16], P('tm'), may hold values from 0.05 to 8
- cosine_weights: float32 [16, 16], replicated, may hold values from -3 to 3
Outputs:
- polar_freq: float32 [16, 4, 1024, 4096], P(None, None, ('row', 'tm'), 'col')
The draws below stay inside these ranges and needn't reach their ends.
All inputs are finite; a program needn't handle non-finite values.
Results may differ from the reference program's by a relative error of at most 0.0033.
Values may be sent and summed in bfloat16 or wider, within the bound.
A program may use at most 64 MiB of HBM per device.

```python
import math
import jax
import jax.numpy as jnp
from jax import lax

NG = 4096
NOCC = 1024
NEMP = 3072
NT = 16
NF = 16
N_COL = 4


def shard_levels(own_key, extent, pieces, low, largest):
    def one(position, blocks):
        steps = jax.random.uniform(jax.random.fold_in(jax.random.fold_in(own_key, 6), position), (blocks,), jnp.float32, low / len(pieces), largest / len(pieces))
        return jnp.repeat(jnp.exp(steps), extent[position] // blocks).reshape((-1,) + (1,) * (len(extent) - position - 1))

    gain = one(*pieces[0])
    for cut in pieces[1:]:
        gain = gain * one(*cut)
    return gain


def normal_values(rng, shape, deviation, reach, cuts=(), kind=jnp.bfloat16):
    loudness = shard_levels(rng, shape, cuts, -0.22, 0.18) if cuts else 1.0
    result = jax.random.normal(rng, shape, jnp.float32) * deviation * loudness
    return jnp.minimum(jnp.maximum(result, -reach), reach).astype(kind)


def setup_inputs(seed: int = 0) -> dict:
    arg_keys = jax.random.split(jax.random.key(seed), 7)
    return {
        "filled_orbitals": normal_values(arg_keys[0], (N_COL, NG // N_COL, NOCC), NOCC ** -0.5, 0.1875, ((0, 4), (1, 8), (2, 16))),
        "empty_orbitals": normal_values(arg_keys[1], (N_COL, NG // N_COL, NEMP), NEMP ** -0.5, 0.109375, ((0, 4), (1, 8), (2, 16))),
        "filled_depth": jnp.clip(jnp.exp(math.log(2.0) - 4.61031033 * jax.random.uniform(arg_keys[2], (NOCC,), jnp.float32) ** shard_levels(arg_keys[2], (NOCC,), ((0, 16),), -0.2, 0.2)), 0.019897461, 2.0).astype(jnp.bfloat16),
        "empty_depth": jnp.clip(jnp.exp(math.log(2.0) - 4.61031033 * jax.random.uniform(arg_keys[3], (NEMP,), jnp.float32) ** shard_levels(arg_keys[3], (NEMP,), ((0, 16),), -0.2, 0.2)), 0.019897461, 2.0).astype(jnp.bfloat16),
        "time_points": jnp.clip(jnp.exp(math.log(8.0) - 5.075174 * jax.random.uniform(arg_keys[4], (NT,), jnp.float32) ** shard_levels(arg_keys[4], (NT,), ((0, 16),), -0.2, 0.2)), 0.05, 8.0),
        "cosine_weights": normal_values(arg_keys[5], (NF, NT), 0.5, 3.0, (), jnp.float32),
    }


def reference(filled_orbitals, empty_orbitals, filled_depth, empty_depth, time_points, cosine_weights):
    phi_filled = filled_orbitals.reshape(NG, NOCC)
    phi_empty = empty_orbitals.reshape(NG, NEMP)
    filled_wide = phi_filled.astype(jnp.float32)
    empty_wide = phi_empty.astype(jnp.float32)
    depth_filled = filled_depth.astype(jnp.float32)
    depth_empty = empty_depth.astype(jnp.float32)

    def one_time(tau_value):
        scaled_filled = (filled_wide * jnp.exp(-depth_filled * tau_value)[None, :]).astype(jnp.bfloat16)
        scaled_empty = (empty_wide * jnp.exp(-depth_empty * tau_value)[None, :]).astype(jnp.bfloat16)
        green_filled = lax.dot_general(filled_wide, scaled_filled.astype(jnp.float32), (((1,), (1,)), ((), ())), precision=lax.Precision.HIGHEST, preferred_element_type=jnp.float32)
        green_empty = lax.dot_general(empty_wide, scaled_empty.astype(jnp.float32), (((1,), (1,)), ((), ())), precision=lax.Precision.HIGHEST, preferred_element_type=jnp.float32)
        return (-(green_filled * green_empty)).astype(jnp.bfloat16)

    polar_time = lax.map(one_time, time_points)
    polar_freq = jnp.einsum("ft,tpq->fpq", cosine_weights, polar_time.astype(jnp.float32), precision=lax.Precision.HIGHEST)
    return polar_freq.reshape(NF, N_COL, NG // N_COL, NG)
```

```python
import jax
import jax.numpy as jnp
from jax import lax
from jax.experimental import pallas as pl
from jax.experimental.pallas import tpu as pltpu
from jax.sharding import PartitionSpec as P

F32 = jnp.float32
BF16 = jnp.bfloat16
MESH = pl.DeviceIdType.MESH
NT_DIMS = (((1,), (1,)), ((), ()))

N_TM = 16
RING = 8
KHALF = 2048
KFILLED = 1024


def offset(i):
    return (1 - 2 * (i % 2)) * ((i + 1) // 2)


def gather_kernel(
    tp_ref, fo_ref, eo_ref, fd_ref, ed_ref, out_ref,
    msg, arrived, blocks, rowblk, dep, expo, scaled, left, ptile,
    s0_send, s0_recv, r_send, r_recv, s1_send, s1_recv, s2_send, s2_recv, p_send, p_recv,
):
    y = lax.axis_index("row")
    col = lax.axis_index("col")
    tm = lax.axis_index("tm")
    x_lo, core = col // 2, col % 2
    x_hi, z = tm // RING, tm % RING
    flip = (1 - x_lo) * 2 + core
    a = z + core * (y - z)
    b = y + core * (z - y)
    mine = x_hi * 4 + flip

    def at(ap, bp):
        return (bp + core * (ap - bp), col, x_hi * RING + ap + core * (bp - ap))

    def plus(v, d):
        return (v + d + 2 * RING) % RING

    a_right, a_left = at(plus(a, 1), b), at(plus(a, -1), b)
    b_right, b_left = at(a, plus(b, 1)), at(a, plus(b, -1))

    def row_device(e):
        q = e % 4
        return (y, (1 - q // 2) * 2 + q % 2, (e // 4) * RING + z)

    barrier = pltpu.get_barrier_semaphore()

    def greet(device):
        pl.semaphore_signal(barrier, inc=1, device_id=device, device_id_type=MESH)

    @pl.loop(0, N_TM)
    def _(t):
        greet((y, flip, t))

    for dev in (a_right, a_left, b_right, b_left):
        greet(dev)
    greet((y, col, (1 - x_hi) * RING + z))
    other = x_lo * 2 + 1 - core
    for xh in range(2):
        greet((y, other, xh * RING + z))
        greet((y, (1 - x_lo) * 2 + 1 - core, xh * RING + z))

    odd = tm % 2
    def arrange(f, e):
        tail = e[:, 128:192]
        low = jnp.concatenate([f, tail], axis=1)
        high = jnp.concatenate([tail, f], axis=1)
        return jnp.where(odd == 1, high, low), e[:, :128]

    f0, f1 = arrange(fo_ref[...].astype(F32), eo_ref[...].astype(F32))
    rows = jnp.concatenate([f0.reshape(N_TM, 8, 128), f1.reshape(N_TM, 8, 128)], axis=1)
    msg[:, 0:16, :] = rows.astype(BF16)
    d0, d1 = arrange(fd_ref[...].astype(F32), ed_ref[...].astype(F32))
    tau = jnp.full((1, 128), tp_ref[0], F32)
    t_hi = tau.astype(BF16).astype(F32)
    t_mid = (tau - t_hi).astype(BF16).astype(F32)
    t_low = tau - t_hi - t_mid
    aux = jnp.concatenate([d0, d1, t_hi, t_mid, t_low, jnp.zeros((11, 128), F32)], axis=0)
    msg[:, 16:32, :] = jnp.broadcast_to(aux.astype(BF16)[None], (N_TM, 16, 128))

    pl.semaphore_wait(barrier, 25)

    def s0_copy(to):
        return pltpu.make_async_remote_copy(
            src_ref=msg.at[to], dst_ref=arrived.at[tm], send_sem=s0_send.at[to],
            recv_sem=s0_recv.at[tm], device_id=(y, flip, to), device_id_type=MESH)

    @pl.loop(0, N_TM)
    def _(t):
        s0_copy((tm + t) % N_TM).start()

    def wait_recv(dst, sem, device):
        pltpu.make_async_remote_copy(
            src_ref=dst, dst_ref=dst, send_sem=sem, recv_sem=sem,
            device_id=device, device_id_type=MESH).wait_recv()

    def wait_send(src, sem, device):
        pltpu.make_async_remote_copy(
            src_ref=src, dst_ref=src, send_sem=sem, recv_sem=sem,
            device_id=device, device_id_type=MESH).wait_send()

    @pl.loop(0, N_TM)
    def _(t):
        wait_recv(arrived.at[t], s0_recv.at[t], b_right)

    lane = lax.broadcasted_iota(jnp.int32, (8, 128), 1)
    first = lane < 64
    for i in range(8):
        even = arrived[2 * i, 0:16, :].astype(F32)[0:8]
        oddb = arrived[2 * i + 1, 0:16, :].astype(F32)[0:8]
        fil = jnp.where(first, even, oddb)
        tail = jnp.where(first, oddb, even)
        m0 = arrived[i, 0:16, :].astype(F32)[8:16]
        m1 = arrived[8 + i, 0:16, :].astype(F32)[8:16]
        lo = jnp.concatenate([fil, m0], axis=0).astype(BF16)
        hi = jnp.concatenate([tail, m1], axis=0).astype(BF16)
        blocks[b, a, :, i * 128:(i + 1) * 128] = lo
        blocks[b, a, :, (8 + i) * 128:(9 + i) * 128] = hi
        rowblk[mine, :, i * 128:(i + 1) * 128] = lo
        rowblk[mine, :, (8 + i) * 128:(9 + i) * 128] = hi

    def s1_copy(i, rightward):
        ref = blocks.at[b, plus(a, offset(i))]
        k = (i + 1) // 2
        landed = 2 * (k + 1) - 1 if rightward else 2 * (k + 1)
        slot = 0 if rightward else 1
        return pltpu.make_async_remote_copy(
            src_ref=ref, dst_ref=ref, send_sem=s1_send.at[slot, k],
            recv_sem=s1_recv.at[landed], device_id=a_right if rightward else a_left,
            device_id_type=MESH)

    def s2_copy(k, i, way):
        bp = plus(b, -k if way == 0 else k)
        ref = blocks.at[bp, plus(a, offset(i))]
        return pltpu.make_async_remote_copy(
            src_ref=ref, dst_ref=ref, send_sem=s2_send.at[way, k, i],
            recv_sem=s2_recv.at[way, k, i], device_id=b_right if way == 0 else b_left,
            device_id_type=MESH)

    def row_copy(j):
        e = (mine + j) % 8
        return pltpu.make_async_remote_copy(
            src_ref=blocks.at[b, a], dst_ref=rowblk.at[mine], send_sem=r_send.at[e],
            recv_sem=r_recv.at[mine], device_id=row_device(e), device_id_type=MESH)

    s1_copy(0, True).start()
    s1_copy(0, False).start()
    s2_copy(0, 0, 0).start()
    s2_copy(0, 0, 1).start()

    @pl.loop(1, 8)
    def _(j):
        row_copy(j).start()

    for i in range(8):
        even = arrived[2 * i, 16:32, :].astype(F32)
        oddb = arrived[2 * i + 1, 16:32, :].astype(F32)
        m0 = arrived[i, 16:32, :].astype(F32)
        m1 = arrived[8 + i, 16:32, :].astype(F32)
        e0 = jnp.broadcast_to(even[0:1], (8, 128))
        o0 = jnp.broadcast_to(oddb[0:1], (8, 128))
        dep[:, i * 128:(i + 1) * 128] = jnp.where(first, e0, o0)
        dep[:, (8 + i) * 128:(9 + i) * 128] = jnp.where(first, o0, e0)
        dep[:, (16 + i) * 128:(17 + i) * 128] = jnp.broadcast_to(m0[1:2], (8, 128))
        dep[:, (24 + i) * 128:(25 + i) * 128] = jnp.broadcast_to(m1[1:2], (8, 128))

    @pl.loop(0, N_TM)
    def _(t):
        info = arrived[t, 16:32, :].astype(F32)
        tv = jnp.broadcast_to(info[2:3] + info[3:4] + info[4:5], (8, 128))
        for g in range(32):
            cut = slice(g * 128, (g + 1) * 128)
            expo[t, :, cut] = jnp.exp(-dep[:, cut] * tv)

    for i in range(1, 8):
        wait_recv(blocks.at[b, plus(a, offset(i))], s1_recv.at[i], a_left)
        if i in (1, 3, 5):
            s1_copy(i, True).start()
        elif i in (2, 4):
            s1_copy(i, False).start()
        s2_copy(0, i, 0).start()
        s2_copy(0, i, 1).start()

    def relay(k, n):
        for half in range(2):
            i = 2 * n + half

            def take(way):
                bp = plus(b, -k if way == 0 else k)
                wait_recv(blocks.at[bp, plus(a, offset(i))], s2_recv.at[way, k - 1, i], b_left)

            def hand(way):
                s2_copy(k, i, way).start()

            if k < 3:
                for way in range(2):
                    take(way)
                    hand(way)
            elif k == 3:
                take(0)
                pl.when(n < 2)(lambda: hand(0))
                take(1)
                pl.when(n >= 2)(lambda: hand(1))
            else:
                pl.when(n < 2)(lambda: take(0))
                pl.when(n >= 2)(lambda: take(1))

    def scale_rows(jj):
        e = (mine + jj) % 8

        @pl.when(jj > 0)
        def _():
            wait_recv(rowblk.at[e], r_recv.at[e], b_left)

        lo = rowblk[e].astype(F32)[0:8]
        hi = rowblk[e].astype(F32)[8:16]

        @pl.loop(0, N_TM // 2)
        def _(tp):
            at_row = pl.ds(pl.multiple_of(e * 128 + tp * 16, 16), 16)
            for part, src in ((0, lo), (1, hi)):
                cut = slice(part * KHALF, (part + 1) * KHALF)
                both = [src * expo[2 * tp + h, :, cut] for h in range(2)]
                scaled[at_row, cut] = jnp.concatenate(both, axis=0).astype(BF16)

    def load_left(slot, r):
        bp = plus(b, offset(r))

        @pl.loop(0, 4)
        def _(j):
            v = blocks[bp, pl.ds(2 * j, 2)].astype(F32)
            at_row = pl.ds(pl.multiple_of(slot * 64 + j * 16, 16), 16)
            left[at_row, 0:KHALF] = v[:, 0:8].reshape(16, KHALF).astype(BF16)
            left[at_row, KHALF:] = v[:, 8:16].reshape(16, KHALF).astype(BF16)

    def p_copy(d, r):
        return pltpu.make_async_remote_copy(
            src_ref=ptile.at[d, r], dst_ref=out_ref.at[x_hi, plus(b, offset(r))],
            send_sem=p_send.at[d, r], recv_sem=p_recv.at[x_hi, r],
            device_id=(y, flip, d * RING + z), device_id_type=MESH)

    def product(rs, n):
        m = 64 * len(rs)
        at_row = pl.ds(pl.multiple_of(n * 256, 256), 256)
        g_o = lax.dot_general(left[0:m, 0:KFILLED], scaled[at_row, 0:KFILLED], NT_DIMS,
                              preferred_element_type=F32)
        g_e = lax.dot_general(left[0:m, KFILLED:], scaled[at_row, KFILLED:], NT_DIMS,
                              preferred_element_type=F32)
        p = (-(g_o * g_e)).astype(BF16)
        d, q = n // 2, 2 * (n % 2)
        for s, r in enumerate(rs):
            for h in range(2):
                ptile[d, r, q + h] = p[s * 64:(s + 1) * 64, h * 128:(h + 1) * 128]

        @pl.when(n % 2 == 1)
        def _():
            for r in rs:
                p_copy(d, r).start()

    @pl.loop(0, 4)
    def _(n):
        relay(1, n)
        scale_rows(2 * n)
        scale_rows(2 * n + 1)

    for k, rs in ((2, (0, 1, 2)), (3, (3, 4)), (4, (5, 6)), (5, (7,))):
        for s, r in enumerate(rs):
            load_left(s, r)

        @pl.loop(0, 4)
        def _(n):
            if k < 5:
                relay(k, n)
            product(rs, n)

    for d in range(2):
        @pl.loop(0, 8)
        def _(r):
            wait_recv(out_ref.at[d, plus(b, offset(r))], p_recv.at[d, r], b_left)

    @pl.loop(0, N_TM)
    def _(t):
        wait_send(msg.at[t], s0_send.at[t], b_left)

    @pl.loop(1, 8)
    def _(j):
        wait_send(blocks.at[b, a], r_send.at[(mine + j) % 8], b_left)

    for slot, count in ((0, 4), (1, 3)):
        for k in range(count):
            wait_send(blocks.at[b, a], s1_send.at[slot, k], b_left)
    for way in range(2):
        for k in range(3):
            @pl.loop(0, 8)
            def _(i):
                wait_send(blocks.at[b, a], s2_send.at[way, k, i], b_left)

        @pl.loop(0, 4)
        def _(i):
            wait_send(blocks.at[b, a], s2_send.at[way, 3, 4 * way + i], b_left)

        @pl.loop(0, 8)
        def _(r):
            wait_send(ptile.at[way, r], p_send.at[way, r], b_left)


def gather_products(tp, fo, eo, fd, ed):
    vmem = pl.BlockSpec(memory_space=pltpu.VMEM)
    dma = pltpu.SemaphoreType.DMA
    return pl.pallas_call(
        gather_kernel,
        out_shape=jax.ShapeDtypeStruct((2, 8, 4, 64, 128), BF16),
        in_specs=[pl.BlockSpec(memory_space=pltpu.SMEM), vmem, vmem, vmem, vmem],
        out_specs=pl.BlockSpec(memory_space=pl.ANY),
        scratch_shapes=[
            pltpu.VMEM((16, 32, 128), BF16),
            pltpu.VMEM((16, 32, 128), BF16),
            pltpu.VMEM((8, 8, 16, KHALF), BF16),
            pltpu.VMEM((8, 16, KHALF), BF16),
            pltpu.VMEM((8, 2 * KHALF), F32),
            pltpu.VMEM((16, 8, 2 * KHALF), F32),
            pltpu.VMEM((1024, 2 * KHALF), BF16),
            pltpu.VMEM((192, 2 * KHALF), BF16),
            pltpu.VMEM((2, 8, 4, 64, 128), BF16),
            dma((16,)), dma((16,)), dma((8,)), dma((8,)), dma((2, 4)), dma((8,)),
            dma((2, 4, 8)), dma((2, 4, 8)), dma((2, 8)), dma((2, 8)),
        ],
        compiler_params=pltpu.CompilerParams(
            collective_id=0, has_side_effects=True, vmem_limit_bytes=40 * 1024 * 1024),
        cost_estimate=pl.CostEstimate(flops=2 * 1024 * 4096 * 512, bytes_accessed=2 ** 22,
                                      transcendentals=2 ** 16),
        name="gather_products",
    )(tp, fo, eo, fd, ed)


def transform_kernel(w_ref, p_ref, out_ref, kw, points):
    core = lax.axis_index("col") % 2

    @pl.when(pl.program_id(0) == 0)
    def _():
        rr = lax.broadcasted_iota(jnp.int32, (128, 16), 0)
        rc = lax.broadcasted_iota(jnp.int32, (128, 16), 1)
        up = jnp.where(rr // 8 == rc, 1.0, 0.0).astype(BF16)
        cr = lax.broadcasted_iota(jnp.int32, (16, 128), 0)
        cc = lax.broadcasted_iota(jnp.int32, (16, 128), 1)
        across = jnp.where(cc // 8 == cr, 1.0, 0.0).astype(BF16)
        r2 = lax.broadcasted_iota(jnp.int32, (128, 128), 0)
        c2 = lax.broadcasted_iota(jnp.int32, (128, 128), 1)
        keep = (r2 % 8) == (c2 % 8)
        rest = w_ref[...]
        for i in range(3):
            part = rest.astype(BF16)
            rest = rest - part.astype(F32)
            tall = jnp.dot(up, part, preferred_element_type=F32).astype(BF16)
            full = jnp.dot(tall, across, preferred_element_type=F32)
            kw[i] = jnp.where(keep, full, 0.0).astype(BF16)

    @pl.when(core == 0)
    def _():
        for n in range(2):
            for yp in range(8):
                points[(2 * yp + n) * 64:(2 * yp + n + 1) * 64, :] = p_ref[n, yp, 0]

    @pl.when(core == 1)
    def _():
        for n in range(2):
            v = p_ref[n, :, 0].astype(F32)
            for yp in range(8):
                piece = v[:, yp * 8:(yp + 1) * 8, :].reshape(64, 128)
                points[(2 * yp + n) * 64:(2 * yp + n + 1) * 64, :] = piece.astype(BF16)

    for c in range(4):
        pts = points[c * 256:(c + 1) * 256, :]
        total = lax.dot_general(kw[2], pts, NT_DIMS, preferred_element_type=F32)
        total += lax.dot_general(kw[1], pts, NT_DIMS, preferred_element_type=F32)
        total += lax.dot_general(kw[0], pts, NT_DIMS, preferred_element_type=F32)
        out_ref[:, 0, :, c * 256:(c + 1) * 256] = total.reshape(16, 8, 256)


def transform(w, p):
    return pl.pallas_call(
        transform_kernel,
        out_shape=jax.ShapeDtypeStruct((16, 4, 8, 1024), F32),
        grid=(4,),
        in_specs=[
            pl.BlockSpec((16, 16), lambda q: (0, 0)),
            pl.BlockSpec((2, 8, 1, 64, 128), lambda q: (0, 0, q, 0, 0)),
        ],
        out_specs=pl.BlockSpec((16, 1, 8, 1024), lambda q: (0, q, 0, 0)),
        scratch_shapes=[pltpu.VMEM((3, 128, 128), BF16), pltpu.VMEM((1024, 128), BF16)],
        compiler_params=pltpu.CompilerParams(vmem_limit_bytes=16 * 1024 * 1024),
        cost_estimate=pl.CostEstimate(flops=2 ** 28, bytes_accessed=3 * 2 ** 20, transcendentals=0),
        name="transform",
    )(w, p)


def on_device(
    filled_orbitals, empty_orbitals, filled_depth, empty_depth, time_points, cosine_weights
):
    p = gather_products(
        time_points,
        filled_orbitals.reshape(128, 64),
        empty_orbitals.reshape(128, 192),
        filled_depth.reshape(1, 64),
        empty_depth.reshape(1, 192),
    )
    return transform(cosine_weights, p)


def solution(mesh):
    in_specs = (P("col", "row", "tm"), P("col", "row", "tm"), P("tm"), P("tm"), P("tm"), P())
    out_specs = P(None, None, ("row", "tm"), "col")
    return jax.shard_map(
        on_device, mesh=mesh, in_specs=in_specs, out_specs=out_specs, check_vma=False
    )
```

```python
import jax
import jax.numpy as jnp
from jax import lax
from jax.experimental import pallas as pl
from jax.experimental.pallas import tpu as pltpu
from jax.sharding import PartitionSpec as P

F32 = jnp.float32
BF16 = jnp.bfloat16
MESH = pl.DeviceIdType.MESH
NT_DIMS = (((1,), (1,)), ((), ()))

N_TM = 16
RING = 8
KHALF = 2048
KFILLED = 1024


def offset(i):
    return (1 - 2 * (i % 2)) * ((i + 1) // 2)


def gather_kernel(
    tp_ref, fo_ref, eo_ref, fd_ref, ed_ref, out_ref,
    fo, eo, fd, ed, msg, arrived, info, infos, blocks, rowblk, dep, expo, scaled, left, ptile,
    in_sem, s0_send, s0_recv, i_send, i_recv, r_send, r_recv, s1_send, s1_recv,
    s2_send, s2_recv, p_send, p_recv,
):
    y = lax.axis_index("row")
    col = lax.axis_index("col")
    tm = lax.axis_index("tm")
    x_lo, core = col // 2, col % 2
    x_hi, z = tm // RING, tm % RING
    flip = (1 - x_lo) * 2 + core
    a = z + core * (y - z)
    b = y + core * (z - y)
    mine = x_hi * 4 + flip

    def at(ap, bp):
        return (bp + core * (ap - bp), col, x_hi * RING + ap + core * (bp - ap))

    def plus(v, d):
        return (v + d + 2 * RING) % RING

    b_right, b_left = at(a, plus(b, 1)), at(a, plus(b, -1))

    group = x_hi * 2 + x_lo
    sibling = (y, x_lo * 2 + 1 - core, tm)

    def row_index(g, c):
        return (g // 2) * 4 + (1 - g % 2) * 2 + c

    loads = [
        pltpu.make_async_copy(src, dst, in_sem.at[i])
        for i, (src, dst) in enumerate(((fo_ref, fo), (eo_ref, eo), (fd_ref, fd), (ed_ref, ed)))
    ]
    for load in loads:
        load.start()

    barrier = pltpu.get_barrier_semaphore()

    def greet(device):
        pl.semaphore_signal(barrier, inc=1, device_id=device, device_id_type=MESH)

    @pl.loop(0, N_TM)
    def _(t):
        greet((y, flip, t))

    greet((plus(y, 1), col, tm))
    greet((plus(y, -1), col, tm))

    @pl.when(core == 1)
    def _():
        for d in (2, -2):
            greet((plus(y, d), col, tm))

    greet(sibling)

    for load in loads:
        load.wait()

    odd = tm % 2

    def arrange(f, e, axis):
        tail = lax.slice_in_dim(e, 128, 192, axis=axis)
        low = jnp.concatenate([f, tail], axis=axis)
        high = jnp.concatenate([tail, f], axis=axis)
        return jnp.where(odd == 1, high, low), lax.slice_in_dim(e, 0, 128, axis=axis)

    f0, f1 = arrange(fo[...].astype(F32), eo[...].astype(F32), 0)
    rows = jnp.concatenate([f0.T.reshape(N_TM, 8, 128), f1.T.reshape(N_TM, 8, 128)], axis=1)
    msg[...] = rows.astype(BF16)

    pl.semaphore_wait(barrier, 19 + 2 * core)

    def s0_copy(to):
        return pltpu.make_async_remote_copy(
            src_ref=msg.at[to], dst_ref=arrived.at[tm], send_sem=s0_send.at[to],
            recv_sem=s0_recv.at[tm], device_id=(y, flip, to), device_id_type=MESH)

    def info_copy(to):
        return pltpu.make_async_remote_copy(
            src_ref=info, dst_ref=infos.at[tm], send_sem=i_send.at[to],
            recv_sem=i_recv.at[tm], device_id=(y, flip, to), device_id_type=MESH)

    @pl.loop(0, N_TM)
    def _(t):
        s0_copy((tm + t) % N_TM).start()

    d0, d1 = arrange(fd[...].astype(F32).reshape(1, 64), ed[...].astype(F32).reshape(1, 192), 1)
    tau = jnp.full((1, 128), tp_ref[0], F32)
    t_hi = tau.astype(BF16).astype(F32)
    t_mid = (tau - t_hi).astype(BF16).astype(F32)
    t_low = tau - t_hi - t_mid
    info[...] = jnp.concatenate(
        [d0, d1, t_hi, t_mid, t_low, jnp.zeros((11, 128), F32)], axis=0).astype(BF16)

    def wait_recv(dst, sem, device):
        pltpu.make_async_remote_copy(
            src_ref=dst, dst_ref=dst, send_sem=sem, recv_sem=sem,
            device_id=device, device_id_type=MESH).wait_recv()

    def wait_send(src, sem, device):
        pltpu.make_async_remote_copy(
            src_ref=src, dst_ref=src, send_sem=sem, recv_sem=sem,
            device_id=device, device_id_type=MESH).wait_send()

    @pl.loop(0, N_TM)
    def _(t):
        wait_recv(arrived.at[t], s0_recv.at[t], b_right)

    lane = lax.broadcasted_iota(jnp.int32, (8, 128), 1)
    first = lane < 64
    for i in range(8):
        even = arrived[2 * i].astype(F32)[0:8]
        oddb = arrived[2 * i + 1].astype(F32)[0:8]
        fil = jnp.where(first, even, oddb)
        tail = jnp.where(first, oddb, even)
        m0 = arrived[i].astype(F32)[8:16]
        m1 = arrived[8 + i].astype(F32)[8:16]
        lo = jnp.concatenate([fil, m0], axis=0).astype(BF16)
        hi = jnp.concatenate([tail, m1], axis=0).astype(BF16)
        blocks[b, a, :, i * 128:(i + 1) * 128] = lo
        blocks[b, a, :, (8 + i) * 128:(9 + i) * 128] = hi
        rowblk[mine, :, i * 128:(i + 1) * 128] = lo
        rowblk[mine, :, (8 + i) * 128:(9 + i) * 128] = hi

    def s1_copy(i, d, seen):
        ref = blocks.at[b, plus(a, offset(i))]
        return pltpu.make_async_remote_copy(
            src_ref=ref, dst_ref=ref, send_sem=s1_send.at[seen], recv_sem=s1_recv.at[seen],
            device_id=at(plus(a, d), b), device_id_type=MESH)

    def s2_copy(k, i, way):
        bp = plus(b, -k if way == 0 else k)
        ref = blocks.at[bp, plus(a, offset(i))]
        return pltpu.make_async_remote_copy(
            src_ref=ref, dst_ref=ref, send_sem=s2_send.at[way, k, i],
            recv_sem=s2_recv.at[way, k, i], device_id=b_right if way == 0 else b_left,
            device_id_type=MESH)

    def row_copy(j):
        g = (group + j) % 4
        return pltpu.make_async_remote_copy(
            src_ref=blocks.at[b, a], dst_ref=rowblk.at[mine], send_sem=r_send.at[j],
            recv_sem=r_recv.at[mine], device_id=(y, (g % 2) * 2 + core, (g // 2) * RING + z),
            device_id_type=MESH)

    def row_hand(j):
        ref = rowblk.at[row_index((group + j) % 4, core)]
        return pltpu.make_async_remote_copy(
            src_ref=ref, dst_ref=ref, send_sem=r_send.at[4 + j],
            recv_sem=r_recv.at[row_index((group + j) % 4, core)], device_id=sibling,
            device_id_type=MESH)

    s2_copy(0, 0, 0).start()
    s2_copy(0, 0, 1).start()
    for d, seen in ((1, 1), (-1, 2), (2, 3), (-2, 4)):
        s1_copy(0, d, seen).start()

    @pl.loop(1, 4)
    def _(j):
        row_copy(j).start()

    row_hand(0).start()

    @pl.loop(0, N_TM)
    def _(t):
        info_copy((tm + t) % N_TM).start()

    for i in range(1, 8):
        wait_recv(blocks.at[b, plus(a, offset(i))], s1_recv.at[i], b_left)
        if i == 3:
            s1_copy(3, 1, 5).start()
            s1_copy(3, 2, 7).start()
        elif i == 4:
            s1_copy(4, -1, 6).start()
        s2_copy(0, i, 0).start()
        s2_copy(0, i, 1).start()

    def relay(k, n):
        for half in range(2):
            i = 2 * n + half

            def take(way):
                bp = plus(b, -k if way == 0 else k)
                wait_recv(blocks.at[bp, plus(a, offset(i))], s2_recv.at[way, k - 1, i], b_left)

            def hand(way):
                s2_copy(k, i, way).start()

            if k < 3:
                for way in range(2):
                    take(way)
                    hand(way)
            elif k == 3:
                take(0)
                pl.when(n < 2)(lambda: hand(0))
                take(1)
                pl.when(n >= 2)(lambda: hand(1))
            else:
                pl.when(n < 2)(lambda: take(0))
                pl.when(n >= 2)(lambda: take(1))

    def scale_rows(e):
        lo = rowblk[e].astype(F32)[0:8]
        hi = rowblk[e].astype(F32)[8:16]

        @pl.loop(0, N_TM // 2)
        def _(tp):
            at_row = pl.ds(pl.multiple_of(e * 128 + tp * 16, 16), 16)
            for part, src in ((0, lo), (1, hi)):
                cut = slice(part * KHALF, (part + 1) * KHALF)
                both = [src * expo[2 * tp + h, :, cut] for h in range(2)]
                scaled[at_row, cut] = jnp.concatenate(both, axis=0).astype(BF16)

    def load_left(slot, r):
        bp = plus(b, offset(r))

        @pl.loop(0, 4)
        def _(j):
            v = blocks[bp, pl.ds(2 * j, 2)].astype(F32)
            at_row = pl.ds(pl.multiple_of(slot * 64 + j * 16, 16), 16)
            left[at_row, 0:KHALF] = v[:, 0:8].reshape(16, KHALF).astype(BF16)
            left[at_row, KHALF:] = v[:, 8:16].reshape(16, KHALF).astype(BF16)

    def p_copy(d, r):
        return pltpu.make_async_remote_copy(
            src_ref=ptile.at[d, r], dst_ref=out_ref.at[x_hi, plus(b, offset(r))],
            send_sem=p_send.at[d, r], recv_sem=p_recv.at[x_hi, r],
            device_id=(y, flip, d * RING + z), device_id_type=MESH)

    def product(rs, n):
        m = 64 * len(rs)
        at_row = pl.ds(pl.multiple_of(n * 256, 256), 256)
        g_o = lax.dot_general(scaled[at_row, 0:KFILLED], left[0:m, 0:KFILLED], NT_DIMS,
                              preferred_element_type=F32)
        g_e = lax.dot_general(scaled[at_row, KFILLED:], left[0:m, KFILLED:], NT_DIMS,
                              preferred_element_type=F32)
        p = (-(g_o * g_e)).T.astype(BF16)
        d, q = n // 2, 2 * (n % 2)
        for s, r in enumerate(rs):
            for h in range(2):
                ptile[d, r, q + h] = p[s * 64:(s + 1) * 64, h * 128:(h + 1) * 128]

        @pl.when(n % 2 == 1)
        def _():
            for r in rs:
                p_copy(d, r).start()

    relay(1, 0)

    @pl.loop(0, N_TM)
    def _(t):
        wait_recv(infos.at[t], i_recv.at[t], b_right)

    for i in range(8):
        even = infos[2 * i].astype(F32)
        oddb = infos[2 * i + 1].astype(F32)
        m0 = infos[i].astype(F32)
        m1 = infos[8 + i].astype(F32)
        e0 = jnp.broadcast_to(even[0:1], (8, 128))
        o0 = jnp.broadcast_to(oddb[0:1], (8, 128))
        dep[:, i * 128:(i + 1) * 128] = jnp.where(first, e0, o0)
        dep[:, (8 + i) * 128:(9 + i) * 128] = jnp.where(first, o0, e0)
        dep[:, (16 + i) * 128:(17 + i) * 128] = jnp.broadcast_to(m0[1:2], (8, 128))
        dep[:, (24 + i) * 128:(25 + i) * 128] = jnp.broadcast_to(m1[1:2], (8, 128))

    @pl.loop(0, N_TM)
    def _(t):
        v = infos[t].astype(F32)
        tv = jnp.broadcast_to(v[2:3] + v[3:4] + v[4:5], (8, 128))
        for g in range(32):
            cut = slice(g * 128, (g + 1) * 128)
            expo[t, :, cut] = jnp.exp(-dep[:, cut] * tv)

    @pl.loop(0, 4)
    def _(n):
        g = (group + n) % 4
        own, other = row_index(g, core), row_index(g, 1 - core)

        @pl.when(n > 0)
        def _():
            wait_recv(rowblk.at[own], r_recv.at[own], b_left)
            row_hand(n).start()

        scale_rows(own)
        wait_recv(rowblk.at[other], r_recv.at[other], b_left)
        scale_rows(other)
        pl.when(n < 3)(lambda: relay(1, n + 1))

    for k, rs in ((2, (0, 1, 2)), (3, (3, 4)), (4, (5, 6)), (5, (7,))):
        for s, r in enumerate(rs):
            load_left(s, r)

        @pl.loop(0, 4)
        def _(n):
            if k < 5:
                relay(k, n)
            product(rs, n)

    for d in range(2):
        @pl.loop(0, 8)
        def _(r):
            wait_recv(out_ref.at[d, plus(b, offset(r))], p_recv.at[d, r], b_left)

    @pl.loop(0, N_TM)
    def _(t):
        wait_send(msg.at[t], s0_send.at[t], b_left)
        wait_send(info, i_send.at[t], b_left)

    @pl.loop(1, 8)
    def _(j):
        wait_send(blocks.at[b, a], r_send.at[j], b_left)
        wait_send(blocks.at[b, a], s1_send.at[j], b_left)

    for way in range(2):
        for k in range(3):
            @pl.loop(0, 8)
            def _(i):
                wait_send(blocks.at[b, a], s2_send.at[way, k, i], b_left)

        @pl.loop(0, 4)
        def _(i):
            wait_send(blocks.at[b, a], s2_send.at[way, 3, 4 * way + i], b_left)

        @pl.loop(0, 8)
        def _(r):
            wait_send(ptile.at[way, r], p_send.at[way, r], b_left)


def gather_products(tp, fo, eo, fd, ed):
    hbm = pl.BlockSpec(memory_space=pltpu.HBM)
    dma = pltpu.SemaphoreType.DMA
    return pl.pallas_call(
        gather_kernel,
        out_shape=jax.ShapeDtypeStruct((2, 8, 4, 64, 128), BF16),
        in_specs=[pl.BlockSpec(memory_space=pltpu.SMEM), hbm, hbm, hbm, hbm],
        out_specs=pl.BlockSpec(memory_space=pl.ANY),
        scratch_shapes=[
            pltpu.VMEM(fo.shape, BF16), pltpu.VMEM(eo.shape, BF16),
            pltpu.VMEM(fd.shape, BF16), pltpu.VMEM(ed.shape, BF16),
            pltpu.VMEM((16, 16, 128), BF16), pltpu.VMEM((16, 16, 128), BF16),
            pltpu.VMEM((16, 128), BF16), pltpu.VMEM((16, 16, 128), BF16),
            pltpu.VMEM((8, 8, 16, KHALF), BF16),
            pltpu.VMEM((8, 16, KHALF), BF16),
            pltpu.VMEM((8, 2 * KHALF), F32),
            pltpu.VMEM((16, 8, 2 * KHALF), F32),
            pltpu.VMEM((1024, 2 * KHALF), BF16),
            pltpu.VMEM((192, 2 * KHALF), BF16),
            pltpu.VMEM((2, 8, 4, 64, 128), BF16),
            dma((4,)), dma((16,)), dma((16,)), dma((16,)), dma((16,)), dma((8,)), dma((8,)),
            dma((8,)), dma((8,)),
            dma((2, 4, 8)), dma((2, 4, 8)), dma((2, 8)), dma((2, 8)),
        ],
        compiler_params=pltpu.CompilerParams(
            collective_id=0, has_side_effects=True, vmem_limit_bytes=60 * 1024 * 1024),
        cost_estimate=pl.CostEstimate(flops=2 * 1024 * 4096 * 512, bytes_accessed=2 ** 22,
                                      transcendentals=2 ** 16),
        name="gather_products",
    )(tp, fo, eo, fd, ed)


def transform_kernel(w_ref, p_ref, out_ref, p, kw, points, result, p_sem, out_sem):
    core = lax.axis_index("col") % 2
    loads = [pltpu.make_async_copy(p_ref.at[:, :, q], p.at[q], p_sem.at[q]) for q in range(4)]
    for load in loads:
        load.start()

    rr = lax.broadcasted_iota(jnp.int32, (128, 16), 0)
    rc = lax.broadcasted_iota(jnp.int32, (128, 16), 1)
    up = jnp.where(rr // 8 == rc, 1.0, 0.0).astype(BF16)
    cr = lax.broadcasted_iota(jnp.int32, (16, 128), 0)
    cc = lax.broadcasted_iota(jnp.int32, (16, 128), 1)
    across = jnp.where(cc // 8 == cr, 1.0, 0.0).astype(BF16)
    r2 = lax.broadcasted_iota(jnp.int32, (128, 128), 0)
    c2 = lax.broadcasted_iota(jnp.int32, (128, 128), 1)
    keep = (r2 % 8) == (c2 % 8)
    rest = w_ref[...]
    for i in range(3):
        part = rest.astype(BF16)
        rest = rest - part.astype(F32)
        tall = jnp.dot(up, part, preferred_element_type=F32).astype(BF16)
        full = jnp.dot(tall, across, preferred_element_type=F32)
        kw[i * 128:(i + 1) * 128, :] = jnp.where(keep, full, 0.0).astype(BF16)

    stores = []
    for q in range(4):
        loads[q].wait()

        @pl.when(core == 0)
        def _():
            for n in range(2):
                for yp in range(8):
                    points[(2 * yp + n) * 64:(2 * yp + n + 1) * 64, :] = p[q, n, yp]

        @pl.when(core == 1)
        def _():
            for n in range(2):
                v = p[q, n].astype(F32)
                for yp in range(8):
                    piece = v[:, yp * 8:(yp + 1) * 8, :].reshape(64, 128)
                    points[(2 * yp + n) * 64:(2 * yp + n + 1) * 64, :] = piece.astype(BF16)

        for c in range(4):
            pts = points[c * 256:(c + 1) * 256, :]
            three = lax.dot_general(kw[...], pts, NT_DIMS, preferred_element_type=F32)
            total = three[256:384] + three[128:256] + three[0:128]
            result[:, q, :, c * 256:(c + 1) * 256] = total.reshape(16, 8, 256)
        store = pltpu.make_async_copy(result.at[:, q], out_ref.at[:, q], out_sem.at[q])
        store.start()
        stores.append(store)
    for store in stores:
        store.wait()


def transform(w, p):
    dma = pltpu.SemaphoreType.DMA
    return pl.pallas_call(
        transform_kernel,
        out_shape=jax.ShapeDtypeStruct((16, 4, 8, 1024), F32),
        in_specs=[pl.BlockSpec(memory_space=pltpu.VMEM), pl.BlockSpec(memory_space=pl.ANY)],
        out_specs=pl.BlockSpec(memory_space=pl.ANY),
        scratch_shapes=[
            pltpu.VMEM((4, 2, 8, 64, 128), BF16), pltpu.VMEM((384, 128), BF16),
            pltpu.VMEM((1024, 128), BF16), pltpu.VMEM((16, 4, 8, 1024), F32), dma((4,)), dma((4,)),
        ],
        compiler_params=pltpu.CompilerParams(vmem_limit_bytes=60 * 1024 * 1024),
        cost_estimate=pl.CostEstimate(flops=2 ** 28, bytes_accessed=3 * 2 ** 20, transcendentals=0),
        name="transform",
    )(w, p)


def on_device(
    filled_orbitals, empty_orbitals, filled_depth, empty_depth, time_points, cosine_weights
):
    p = gather_products(
        time_points,
        jnp.swapaxes(filled_orbitals, 1, 2).reshape(64, 128),
        jnp.swapaxes(empty_orbitals, 1, 2).reshape(192, 128),
        filled_depth,
        empty_depth,
    )
    return transform(cosine_weights, p)


def solution(mesh):
    in_specs = (P("col", "row", "tm"), P("col", "row", "tm"), P("tm"), P("tm"), P("tm"), P())
    out_specs = P(None, None, ("row", "tm"), "col")
    return jax.shard_map(
        on_device, mesh=mesh, in_specs=in_specs, out_specs=out_specs, check_vma=False
    )
```

```python
import jax
import jax.numpy as jnp
from jax import lax
from jax.experimental import pallas as pl
from jax.experimental.pallas import tpu as pltpu
from jax.sharding import PartitionSpec as P

F32 = jnp.float32
BF16 = jnp.bfloat16
MESH = pl.DeviceIdType.MESH
NT_DIMS = (((1,), (1,)), ((), ()))

N_TM = 16
RING = 8
KHALF = 2048
KFILLED = 1024


def offset(i):
    return (1 - 2 * (i % 2)) * ((i + 1) // 2)


def gather_kernel(
    tp_ref, fo_ref, eo_ref, fd_ref, ed_ref, out_ref,
    fo, eo, fd, ed, msg, arrived, info, infos, blocks, rowblk, dep, expo, scaled, left, ptile,
    in_sem, s0_send, s0_recv, i_send, i_recv, r_send, r_recv, s1_send, s1_recv,
    s2_send, s2_recv, p_send, p_recv,
):
    y = lax.axis_index("row")
    col = lax.axis_index("col")
    tm = lax.axis_index("tm")
    x_lo, core = col // 2, col % 2
    x_hi, z = tm // RING, tm % RING
    flip = (1 - x_lo) * 2 + core
    a = z + core * (y - z)
    b = y + core * (z - y)
    mine = x_hi * 4 + flip

    def at(ap, bp):
        return (bp + core * (ap - bp), col, x_hi * RING + ap + core * (bp - ap))

    def plus(v, d):
        return (v + d + 2 * RING) % RING

    b_right, b_left = at(a, plus(b, 1)), at(a, plus(b, -1))

    group = x_hi * 2 + x_lo
    sibling = (y, x_lo * 2 + 1 - core, tm)

    def row_index(g, c):
        return (g // 2) * 4 + (1 - g % 2) * 2 + c

    loads = [
        pltpu.make_async_copy(src, dst, in_sem.at[i])
        for i, (src, dst) in enumerate(((fo_ref, fo), (eo_ref, eo), (fd_ref, fd), (ed_ref, ed)))
    ]
    for load in loads:
        load.start()

    barrier = pltpu.get_barrier_semaphore()

    def greet(device):
        pl.semaphore_signal(barrier, inc=1, device_id=device, device_id_type=MESH)

    def far(t):
        return (t % 2) * RING + plus(z, 4 + offset(t // 2))

    @pl.loop(0, N_TM)
    def _(t):
        greet((y, flip, far(t)))

    greet((plus(y, 1), col, tm))
    greet((plus(y, -1), col, tm))

    @pl.when(core == 1)
    def _():
        for d in (2, -2):
            greet((plus(y, d), col, tm))

    greet(sibling)

    for load in loads:
        load.wait()

    odd = tm % 2

    def arrange(f, e, axis):
        tail = lax.slice_in_dim(e, 128, 192, axis=axis)
        low = jnp.concatenate([f, tail], axis=axis)
        high = jnp.concatenate([tail, f], axis=axis)
        return jnp.where(odd == 1, high, low), lax.slice_in_dim(e, 0, 128, axis=axis)

    f0, f1 = arrange(fo[...].astype(F32), eo[...].astype(F32), 0)
    rows = jnp.concatenate([f0.T.reshape(N_TM, 8, 128), f1.T.reshape(N_TM, 8, 128)], axis=1)
    msg[...] = rows.astype(BF16)

    pl.semaphore_wait(barrier, 19 + 2 * core)

    def s0_copy(to):
        return pltpu.make_async_remote_copy(
            src_ref=msg.at[to], dst_ref=arrived.at[tm], send_sem=s0_send.at[to],
            recv_sem=s0_recv.at[tm], device_id=(y, flip, to), device_id_type=MESH)

    def info_copy(to):
        return pltpu.make_async_remote_copy(
            src_ref=info, dst_ref=infos.at[tm], send_sem=i_send.at[to],
            recv_sem=i_recv.at[tm], device_id=(y, flip, to), device_id_type=MESH)

    @pl.loop(0, N_TM)
    def _(t):
        s0_copy(far(t)).start()

    d0, d1 = arrange(fd[...].astype(F32).reshape(1, 64), ed[...].astype(F32).reshape(1, 192), 1)
    tau = jnp.full((1, 128), tp_ref[0], F32)
    t_hi = tau.astype(BF16).astype(F32)
    t_mid = (tau - t_hi).astype(BF16).astype(F32)
    t_low = tau - t_hi - t_mid
    info[...] = jnp.concatenate(
        [d0, d1, t_hi, t_mid, t_low, jnp.zeros((11, 128), F32)], axis=0).astype(BF16)

    def wait_recv(dst, sem, device):
        pltpu.make_async_remote_copy(
            src_ref=dst, dst_ref=dst, send_sem=sem, recv_sem=sem,
            device_id=device, device_id_type=MESH).wait_recv()

    def wait_send(src, sem, device):
        pltpu.make_async_remote_copy(
            src_ref=src, dst_ref=src, send_sem=sem, recv_sem=sem,
            device_id=device, device_id_type=MESH).wait_send()

    @pl.loop(0, N_TM)
    def _(t):
        wait_recv(arrived.at[t], s0_recv.at[t], b_right)

    lane = lax.broadcasted_iota(jnp.int32, (8, 128), 1)
    first = lane < 64
    for i in range(8):
        even = arrived[2 * i].astype(F32)[0:8]
        oddb = arrived[2 * i + 1].astype(F32)[0:8]
        fil = jnp.where(first, even, oddb)
        tail = jnp.where(first, oddb, even)
        m0 = arrived[i].astype(F32)[8:16]
        m1 = arrived[8 + i].astype(F32)[8:16]
        lo = jnp.concatenate([fil, m0], axis=0).astype(BF16)
        hi = jnp.concatenate([tail, m1], axis=0).astype(BF16)
        blocks[b, a, :, i * 128:(i + 1) * 128] = lo
        blocks[b, a, :, (8 + i) * 128:(9 + i) * 128] = hi
        rowblk[mine, :, i * 128:(i + 1) * 128] = lo
        rowblk[mine, :, (8 + i) * 128:(9 + i) * 128] = hi

    def s1_copy(i, d, seen):
        ref = blocks.at[b, plus(a, offset(i))]
        return pltpu.make_async_remote_copy(
            src_ref=ref, dst_ref=ref, send_sem=s1_send.at[seen], recv_sem=s1_recv.at[seen],
            device_id=at(plus(a, d), b), device_id_type=MESH)

    def s2_copy(k, i, way):
        bp = plus(b, -k if way == 0 else k)
        ref = blocks.at[bp, plus(a, offset(i))]
        return pltpu.make_async_remote_copy(
            src_ref=ref, dst_ref=ref, send_sem=s2_send.at[way, k, i],
            recv_sem=s2_recv.at[way, k, i], device_id=b_right if way == 0 else b_left,
            device_id_type=MESH)

    def row_copy(j):
        g = (group + j) % 4
        return pltpu.make_async_remote_copy(
            src_ref=blocks.at[b, a], dst_ref=rowblk.at[mine], send_sem=r_send.at[j],
            recv_sem=r_recv.at[mine], device_id=(y, (g % 2) * 2 + core, (g // 2) * RING + z),
            device_id_type=MESH)

    def row_hand(j):
        ref = rowblk.at[row_index((group + j) % 4, core)]
        return pltpu.make_async_remote_copy(
            src_ref=ref, dst_ref=ref, send_sem=r_send.at[4 + j],
            recv_sem=r_recv.at[row_index((group + j) % 4, core)], device_id=sibling,
            device_id_type=MESH)

    s2_copy(0, 0, 0).start()
    s2_copy(0, 0, 1).start()
    for d, seen in ((1, 1), (-1, 2), (2, 3), (-2, 4)):
        s1_copy(0, d, seen).start()

    @pl.loop(1, 4)
    def _(j):
        row_copy(j).start()

    row_hand(0).start()

    @pl.loop(0, N_TM)
    def _(t):
        info_copy(far(t)).start()

    for i in range(1, 8):
        wait_recv(blocks.at[b, plus(a, offset(i))], s1_recv.at[i], b_left)
        if i == 3:
            s1_copy(3, 1, 5).start()
            s1_copy(3, 2, 7).start()
        elif i == 4:
            s1_copy(4, -1, 6).start()
        s2_copy(0, i, 0).start()
        s2_copy(0, i, 1).start()

    def relay(k, n):
        for half in range(2):
            i = 2 * n + half

            def take(way):
                bp = plus(b, -k if way == 0 else k)
                wait_recv(blocks.at[bp, plus(a, offset(i))], s2_recv.at[way, k - 1, i], b_left)

            def hand(way):
                s2_copy(k, i, way).start()

            if k < 3:
                for way in range(2):
                    take(way)
                    hand(way)
            elif k == 3:
                take(0)
                pl.when(n < 2)(lambda: hand(0))
                take(1)
                pl.when(n >= 2)(lambda: hand(1))
            else:
                pl.when(n < 2)(lambda: take(0))
                pl.when(n >= 2)(lambda: take(1))

    def scale_rows(e):
        lo = rowblk[e].astype(F32)[0:8]
        hi = rowblk[e].astype(F32)[8:16]

        @pl.loop(0, N_TM // 2)
        def _(tp):
            at_row = pl.ds(pl.multiple_of(e * 128 + tp * 16, 16), 16)
            for part, src in ((0, lo), (1, hi)):
                cut = slice(part * KHALF, (part + 1) * KHALF)
                both = [src * expo[2 * tp + h, :, cut] for h in range(2)]
                scaled[at_row, cut] = jnp.concatenate(both, axis=0).astype(BF16)

    def load_left(slot, r):
        bp = plus(b, offset(r))

        @pl.loop(0, 4)
        def _(j):
            v = blocks[bp, pl.ds(2 * j, 2)].astype(F32)
            at_row = pl.ds(pl.multiple_of(slot * 64 + j * 16, 16), 16)
            left[at_row, 0:KHALF] = v[:, 0:8].reshape(16, KHALF).astype(BF16)
            left[at_row, KHALF:] = v[:, 8:16].reshape(16, KHALF).astype(BF16)

    def p_copy(d, r, h):
        two = pl.ds(2 * h, 2)
        return pltpu.make_async_remote_copy(
            src_ref=ptile.at[d, r, two], dst_ref=out_ref.at[x_hi, plus(b, offset(r)), two],
            send_sem=p_send.at[d, r, h], recv_sem=p_recv.at[x_hi, r, h],
            device_id=(y, flip, d * RING + z), device_id_type=MESH)

    def product(rs, n):
        m = 64 * len(rs)
        at_row = pl.ds(pl.multiple_of(n * 256, 256), 256)
        g_o = lax.dot_general(scaled[at_row, 0:KFILLED], left[0:m, 0:KFILLED], NT_DIMS,
                              preferred_element_type=F32)
        g_e = lax.dot_general(scaled[at_row, KFILLED:], left[0:m, KFILLED:], NT_DIMS,
                              preferred_element_type=F32)
        p = (-(g_o * g_e)).T.astype(BF16)
        d, q = n // 2, 2 * (n % 2)
        for s, r in enumerate(rs):
            for h in range(2):
                ptile[d, r, q + h] = p[s * 64:(s + 1) * 64, h * 128:(h + 1) * 128]

        for r in rs:
            p_copy(d, r, n % 2).start()

    relay(1, 0)

    @pl.loop(0, N_TM)
    def _(t):
        wait_recv(infos.at[t], i_recv.at[t], b_right)

    for i in range(8):
        even = infos[2 * i].astype(F32)
        oddb = infos[2 * i + 1].astype(F32)
        m0 = infos[i].astype(F32)
        m1 = infos[8 + i].astype(F32)
        e0 = jnp.broadcast_to(even[0:1], (8, 128))
        o0 = jnp.broadcast_to(oddb[0:1], (8, 128))
        dep[:, i * 128:(i + 1) * 128] = jnp.where(first, e0, o0)
        dep[:, (8 + i) * 128:(9 + i) * 128] = jnp.where(first, o0, e0)
        dep[:, (16 + i) * 128:(17 + i) * 128] = jnp.broadcast_to(m0[1:2], (8, 128))
        dep[:, (24 + i) * 128:(25 + i) * 128] = jnp.broadcast_to(m1[1:2], (8, 128))

    @pl.loop(0, N_TM)
    def _(t):
        v = infos[t].astype(F32)
        tv = jnp.broadcast_to(v[2:3] + v[3:4] + v[4:5], (8, 128))
        for g in range(32):
            cut = slice(g * 128, (g + 1) * 128)
            expo[t, :, cut] = jnp.exp(-dep[:, cut] * tv)

    @pl.loop(0, 4)
    def _(n):
        g = (group + n) % 4
        own, other = row_index(g, core), row_index(g, 1 - core)

        @pl.when(n > 0)
        def _():
            wait_recv(rowblk.at[own], r_recv.at[own], b_left)
            row_hand(n).start()

        scale_rows(own)
        wait_recv(rowblk.at[other], r_recv.at[other], b_left)
        scale_rows(other)
        pl.when(n < 3)(lambda: relay(1, n + 1))

    for k, rs in ((2, (0, 1, 2)), (3, (3, 4)), (4, (5, 6)), (5, (7,))):
        for s, r in enumerate(rs):
            load_left(s, r)

        @pl.loop(0, 4)
        def _(n):
            if k < 5:
                relay(k, n)
            product(rs, n)

    for d in range(2):
        @pl.loop(0, 8)
        def _(r):
            for h in range(2):
                wait_recv(out_ref.at[d, plus(b, offset(r)), 2 * h:2 * h + 2], p_recv.at[d, r, h], b_left)

    @pl.loop(0, N_TM)
    def _(t):
        wait_send(msg.at[t], s0_send.at[t], b_left)
        wait_send(info, i_send.at[t], b_left)

    @pl.loop(1, 8)
    def _(j):
        wait_send(blocks.at[b, a], r_send.at[j], b_left)
        wait_send(blocks.at[b, a], s1_send.at[j], b_left)

    for way in range(2):
        for k in range(3):
            @pl.loop(0, 8)
            def _(i):
                wait_send(blocks.at[b, a], s2_send.at[way, k, i], b_left)

        @pl.loop(0, 4)
        def _(i):
            wait_send(blocks.at[b, a], s2_send.at[way, 3, 4 * way + i], b_left)

        @pl.loop(0, 8)
        def _(r):
            for h in range(2):
                wait_send(ptile.at[way, r, 2 * h:2 * h + 2], p_send.at[way, r, h], b_left)


def gather_products(tp, fo, eo, fd, ed):
    hbm = pl.BlockSpec(memory_space=pltpu.HBM)
    dma = pltpu.SemaphoreType.DMA
    return pl.pallas_call(
        gather_kernel,
        out_shape=jax.ShapeDtypeStruct((2, 8, 4, 64, 128), BF16),
        in_specs=[pl.BlockSpec(memory_space=pltpu.SMEM), hbm, hbm, hbm, hbm],
        out_specs=pl.BlockSpec(memory_space=pl.ANY),
        scratch_shapes=[
            pltpu.VMEM(fo.shape, BF16), pltpu.VMEM(eo.shape, BF16),
            pltpu.VMEM(fd.shape, BF16), pltpu.VMEM(ed.shape, BF16),
            pltpu.VMEM((16, 16, 128), BF16), pltpu.VMEM((16, 16, 128), BF16),
            pltpu.VMEM((16, 128), BF16), pltpu.VMEM((16, 16, 128), BF16),
            pltpu.VMEM((8, 8, 16, KHALF), BF16),
            pltpu.VMEM((8, 16, KHALF), BF16),
            pltpu.VMEM((8, 2 * KHALF), F32),
            pltpu.VMEM((16, 8, 2 * KHALF), F32),
            pltpu.VMEM((1024, 2 * KHALF), BF16),
            pltpu.VMEM((192, 2 * KHALF), BF16),
            pltpu.VMEM((2, 8, 4, 64, 128), BF16),
            dma((4,)), dma((16,)), dma((16,)), dma((16,)), dma((16,)), dma((8,)), dma((8,)),
            dma((8,)), dma((8,)),
            dma((2, 4, 8)), dma((2, 4, 8)), dma((2, 8, 2)), dma((2, 8, 2)),
        ],
        compiler_params=pltpu.CompilerParams(
            collective_id=0, has_side_effects=True, vmem_limit_bytes=36 * 1024 * 1024),
        cost_estimate=pl.CostEstimate(flops=2 * 1024 * 4096 * 512, bytes_accessed=2 ** 22,
                                      transcendentals=2 ** 16),
        name="gather_products",
    )(tp, fo, eo, fd, ed)


def transform_kernel(w_ref, p_ref, out_ref, kw, points, result, out_sem):
    core = lax.axis_index("col") % 2
    rr = lax.broadcasted_iota(jnp.int32, (128, 16), 0)
    rc = lax.broadcasted_iota(jnp.int32, (128, 16), 1)
    up = jnp.where(rr // 8 == rc, 1.0, 0.0).astype(BF16)
    cr = lax.broadcasted_iota(jnp.int32, (16, 128), 0)
    cc = lax.broadcasted_iota(jnp.int32, (16, 128), 1)
    across = jnp.where(cc // 8 == cr, 1.0, 0.0).astype(BF16)
    r2 = lax.broadcasted_iota(jnp.int32, (128, 128), 0)
    c2 = lax.broadcasted_iota(jnp.int32, (128, 128), 1)
    keep = (r2 % 8) == (c2 % 8)
    rest = w_ref[...]
    for i in range(3):
        part = rest.astype(BF16)
        rest = rest - part.astype(F32)
        tall = jnp.dot(up, part, preferred_element_type=F32).astype(BF16)
        full = jnp.dot(tall, across, preferred_element_type=F32)
        kw[i * 128:(i + 1) * 128, :] = jnp.where(keep, full, 0.0).astype(BF16)

    stores = []
    for q in range(4):
        @pl.when(core == 0)
        def _():
            for n in range(2):
                for yp in range(8):
                    points[(2 * yp + n) * 64:(2 * yp + n + 1) * 64, :] = p_ref[n, yp, q]

        @pl.when(core == 1)
        def _():
            for n in range(2):
                v = p_ref[n, :, q].astype(F32)
                for yp in range(8):
                    piece = v[:, yp * 8:(yp + 1) * 8, :].reshape(64, 128)
                    points[(2 * yp + n) * 64:(2 * yp + n + 1) * 64, :] = piece.astype(BF16)

        for c in range(4):
            pts = points[c * 256:(c + 1) * 256, :]
            three = lax.dot_general(kw[...], pts, NT_DIMS, preferred_element_type=F32)
            total = three[256:384] + three[128:256] + three[0:128]
            result[:, q, :, c * 256:(c + 1) * 256] = total.reshape(16, 8, 256)
        store = pltpu.make_async_copy(result.at[:, q], out_ref.at[:, q], out_sem.at[q])
        store.start()
        stores.append(store)
    for store in stores:
        store.wait()


def transform(w, p):
    dma = pltpu.SemaphoreType.DMA
    return pl.pallas_call(
        transform_kernel,
        out_shape=jax.ShapeDtypeStruct((16, 4, 8, 1024), F32),
        in_specs=[pl.BlockSpec(memory_space=pltpu.VMEM)] * 2,
        out_specs=pl.BlockSpec(memory_space=pl.ANY),
        scratch_shapes=[
            pltpu.VMEM((384, 128), BF16), pltpu.VMEM((1024, 128), BF16),
            pltpu.VMEM((16, 4, 8, 1024), F32), dma((4,)),
        ],
        compiler_params=pltpu.CompilerParams(vmem_limit_bytes=36 * 1024 * 1024),
        cost_estimate=pl.CostEstimate(flops=2 ** 28, bytes_accessed=3 * 2 ** 20, transcendentals=0),
        name="transform",
    )(w, p)


def on_device(
    filled_orbitals, empty_orbitals, filled_depth, empty_depth, time_points, cosine_weights
):
    def hold(v):
        return pltpu.with_memory_space_constraint(v, pltpu.HBM)

    p = gather_products(
        time_points,
        hold(jnp.swapaxes(filled_orbitals, 1, 2).reshape(64, 128)),
        hold(jnp.swapaxes(empty_orbitals, 1, 2).reshape(192, 128)),
        hold(filled_depth),
        hold(empty_depth),
    )
    return transform(cosine_weights, p)


def solution(mesh):
    in_specs = (P("col", "row", "tm"), P("col", "row", "tm"), P("tm"), P("tm"), P("tm"), P())
    out_specs = P(None, None, ("row", "tm"), "col")
    return jax.shard_map(
        on_device, mesh=mesh, in_specs=in_specs, out_specs=out_specs, check_vma=False
    )
```

```python
import jax
import jax.numpy as jnp
from jax import lax
from jax.experimental import pallas as pl
from jax.experimental.pallas import tpu as pltpu
from jax.sharding import PartitionSpec as P

F32 = jnp.float32
BF16 = jnp.bfloat16
MESH = pl.DeviceIdType.MESH
NT_DIMS = (((1,), (1,)), ((), ()))

N_TM = 16
RING = 8
KHALF = 2048
KFILLED = 1024


def offset(i):
    return (1 - 2 * (i % 2)) * ((i + 1) // 2)


def gather_kernel(
    tp_ref, fo_ref, eo_ref, fd_ref, ed_ref, out_ref,
    fo, eo, fd, ed, msg, arrived, info, infos, blocks, rowblk, dep, expo, scaled, left, ptile,
    in_sem, s0_send, s0_recv, i_send, i_recv, r_send, r_recv, s1_send, s1_recv,
    s2_send, s2_recv, p_send, p_recv,
):
    y = lax.axis_index("row")
    col = lax.axis_index("col")
    tm = lax.axis_index("tm")
    x_lo, core = col // 2, col % 2
    x_hi, z = tm // RING, tm % RING
    flip = (1 - x_lo) * 2 + core
    a = z + core * (y - z)
    b = y + core * (z - y)
    mine = x_hi * 4 + flip

    def at(ap, bp):
        return (bp + core * (ap - bp), col, x_hi * RING + ap + core * (bp - ap))

    def plus(v, d):
        return (v + d + 2 * RING) % RING

    b_right, b_left = at(a, plus(b, 1)), at(a, plus(b, -1))

    group = x_hi * 2 + x_lo
    sibling = (y, x_lo * 2 + 1 - core, tm)

    def row_index(g, c):
        return (g // 2) * 4 + (1 - g % 2) * 2 + c

    loads = [
        pltpu.make_async_copy(src, dst, in_sem.at[i])
        for i, (src, dst) in enumerate(((fo_ref, fo), (eo_ref, eo), (fd_ref, fd), (ed_ref, ed)))
    ]
    for load in loads:
        load.start()

    barrier = pltpu.get_barrier_semaphore()

    def greet(device):
        pl.semaphore_signal(barrier, inc=1, device_id=device, device_id_type=MESH)

    def far(t):
        return (t % 2) * RING + plus(z, 4 + offset(t // 2))

    @pl.loop(0, N_TM)
    def _(t):
        greet((y, flip, far(t)))

    greet((plus(y, 1), col, tm))
    greet((plus(y, -1), col, tm))

    @pl.when(core == 1)
    def _():
        for d in (2, -2):
            greet((plus(y, d), col, tm))

    greet(sibling)

    for load in loads:
        load.wait()

    odd = tm % 2

    def arrange(f, e, axis):
        tail = lax.slice_in_dim(e, 128, 192, axis=axis)
        low = jnp.concatenate([f, tail], axis=axis)
        high = jnp.concatenate([tail, f], axis=axis)
        return jnp.where(odd == 1, high, low), lax.slice_in_dim(e, 0, 128, axis=axis)

    f0, f1 = arrange(fo[...].astype(F32), eo[...].astype(F32), 0)
    rows = jnp.concatenate([f0.T.reshape(N_TM, 8, 128), f1.T.reshape(N_TM, 8, 128)], axis=1)
    msg[...] = rows.astype(BF16)

    pl.semaphore_wait(barrier, 19 + 2 * core)

    def s0_copy(to):
        return pltpu.make_async_remote_copy(
            src_ref=msg.at[to], dst_ref=arrived.at[tm], send_sem=s0_send.at[to],
            recv_sem=s0_recv.at[tm], device_id=(y, flip, to), device_id_type=MESH)

    def info_copy(to):
        return pltpu.make_async_remote_copy(
            src_ref=info, dst_ref=infos.at[tm], send_sem=i_send.at[to],
            recv_sem=i_recv.at[tm], device_id=(y, flip, to), device_id_type=MESH)

    @pl.loop(0, N_TM)
    def _(t):
        s0_copy(far(t)).start()

    d0, d1 = arrange(fd[...].astype(F32).reshape(1, 64), ed[...].astype(F32).reshape(1, 192), 1)
    tau = jnp.full((1, 128), tp_ref[0], F32)
    t_hi = tau.astype(BF16).astype(F32)
    t_mid = (tau - t_hi).astype(BF16).astype(F32)
    t_low = tau - t_hi - t_mid
    info[...] = jnp.concatenate(
        [d0, d1, t_hi, t_mid, t_low, jnp.zeros((11, 128), F32)], axis=0).astype(BF16)

    def wait_recv(dst, sem, device):
        pltpu.make_async_remote_copy(
            src_ref=dst, dst_ref=dst, send_sem=sem, recv_sem=sem,
            device_id=device, device_id_type=MESH).wait_recv()

    def wait_send(src, sem, device):
        pltpu.make_async_remote_copy(
            src_ref=src, dst_ref=src, send_sem=sem, recv_sem=sem,
            device_id=device, device_id_type=MESH).wait_send()

    @pl.loop(0, N_TM)
    def _(t):
        wait_recv(arrived.at[t], s0_recv.at[t], b_right)

    lane = lax.broadcasted_iota(jnp.int32, (8, 128), 1)
    first = lane < 64
    for i in range(8):
        even = arrived[2 * i].astype(F32)[0:8]
        oddb = arrived[2 * i + 1].astype(F32)[0:8]
        fil = jnp.where(first, even, oddb)
        tail = jnp.where(first, oddb, even)
        m0 = arrived[i].astype(F32)[8:16]
        m1 = arrived[8 + i].astype(F32)[8:16]
        lo = jnp.concatenate([fil, m0], axis=0).astype(BF16)
        hi = jnp.concatenate([tail, m1], axis=0).astype(BF16)
        blocks[b, a, :, i * 128:(i + 1) * 128] = lo
        blocks[b, a, :, (8 + i) * 128:(9 + i) * 128] = hi
        rowblk[mine, :, i * 128:(i + 1) * 128] = lo
        rowblk[mine, :, (8 + i) * 128:(9 + i) * 128] = hi

    def s1_copy(i, d, seen):
        ref = blocks.at[b, plus(a, offset(i))]
        return pltpu.make_async_remote_copy(
            src_ref=ref, dst_ref=ref, send_sem=s1_send.at[seen], recv_sem=s1_recv.at[seen],
            device_id=at(plus(a, d), b), device_id_type=MESH)

    def s2_copy(k, i, way):
        bp = plus(b, -k if way == 0 else k)
        ref = blocks.at[bp, plus(a, offset(i))]
        return pltpu.make_async_remote_copy(
            src_ref=ref, dst_ref=ref, send_sem=s2_send.at[way, k, i],
            recv_sem=s2_recv.at[way, k, i], device_id=b_right if way == 0 else b_left,
            device_id_type=MESH)

    def row_copy(j):
        g = (group + j) % 4
        return pltpu.make_async_remote_copy(
            src_ref=blocks.at[b, a], dst_ref=rowblk.at[mine], send_sem=r_send.at[j],
            recv_sem=r_recv.at[mine], device_id=(y, (g % 2) * 2 + core, (g // 2) * RING + z),
            device_id_type=MESH)

    def row_hand(j):
        ref = rowblk.at[row_index((group + j) % 4, core)]
        return pltpu.make_async_remote_copy(
            src_ref=ref, dst_ref=ref, send_sem=r_send.at[4 + j],
            recv_sem=r_recv.at[row_index((group + j) % 4, core)], device_id=sibling,
            device_id_type=MESH)

    s2_copy(0, 0, 0).start()
    s2_copy(0, 0, 1).start()
    for d, seen in ((1, 1), (-1, 2), (2, 3), (-2, 4)):
        s1_copy(0, d, seen).start()

    @pl.loop(1, 4)
    def _(j):
        row_copy(j).start()

    row_hand(0).start()

    @pl.loop(0, N_TM)
    def _(t):
        info_copy(far(t)).start()

    def relay(k, n):
        for half in range(2):
            i = 2 * n + half

            def take(way):
                bp = plus(b, -k if way == 0 else k)
                wait_recv(blocks.at[bp, plus(a, offset(i))], s2_recv.at[way, k - 1, i], b_left)

            def hand(way):
                s2_copy(k, i, way).start()

            if k < 3:
                for way in range(2):
                    take(way)
                    hand(way)
            elif k == 3:
                take(0)
                pl.when(n < 2)(lambda: hand(0))
                take(1)
                pl.when(n >= 2)(lambda: hand(1))
            else:
                pl.when(n < 2)(lambda: take(0))
                pl.when(n >= 2)(lambda: take(1))

    def scale_rows(e):
        lo = rowblk[e].astype(F32)[0:8]
        hi = rowblk[e].astype(F32)[8:16]

        @pl.loop(0, N_TM // 2)
        def _(tp):
            at_row = pl.ds(pl.multiple_of(e * 128 + tp * 16, 16), 16)
            for part, src in ((0, lo), (1, hi)):
                cut = slice(part * KHALF, (part + 1) * KHALF)
                both = [src * expo[2 * tp + h, :, cut] for h in range(2)]
                scaled[at_row, cut] = jnp.concatenate(both, axis=0).astype(BF16)

    def load_left(slot, r):
        bp = plus(b, offset(r))

        @pl.loop(0, 4)
        def _(j):
            v = blocks[bp, pl.ds(2 * j, 2)].astype(F32)
            at_row = pl.ds(pl.multiple_of(slot * 64 + j * 16, 16), 16)
            left[at_row, 0:KHALF] = v[:, 0:8].reshape(16, KHALF).astype(BF16)
            left[at_row, KHALF:] = v[:, 8:16].reshape(16, KHALF).astype(BF16)

    def p_copy(d, r, h):
        two = pl.ds(2 * h, 2)
        return pltpu.make_async_remote_copy(
            src_ref=ptile.at[d, r, two], dst_ref=out_ref.at[x_hi, plus(b, offset(r)), two],
            send_sem=p_send.at[d, r, h], recv_sem=p_recv.at[x_hi, r, h],
            device_id=(y, flip, d * RING + z), device_id_type=MESH)

    def product(rs, n):
        m = 64 * len(rs)
        at_row = pl.ds(pl.multiple_of(n * 256, 256), 256)
        g_o = lax.dot_general(scaled[at_row, 0:KFILLED], left[0:m, 0:KFILLED], NT_DIMS,
                              preferred_element_type=F32)
        g_e = lax.dot_general(scaled[at_row, KFILLED:], left[0:m, KFILLED:], NT_DIMS,
                              preferred_element_type=F32)
        p = (-(g_o * g_e)).T.astype(BF16)
        d, q = n // 2, 2 * (n % 2)
        for s, r in enumerate(rs):
            for h in range(2):
                ptile[d, r, q + h] = p[s * 64:(s + 1) * 64, h * 128:(h + 1) * 128]

        for r in rs:
            p_copy(d, r, n % 2).start()

    for i in range(1, 8):
        wait_recv(blocks.at[b, plus(a, offset(i))], s1_recv.at[i], b_left)
        if i == 3:
            s1_copy(3, 1, 5).start()
            s1_copy(3, 2, 7).start()
        elif i == 4:
            s1_copy(4, -1, 6).start()
        s2_copy(0, i, 0).start()
        s2_copy(0, i, 1).start()
        if i == 4:
            relay(1, 0)


    @pl.loop(0, N_TM)
    def _(t):
        wait_recv(infos.at[t], i_recv.at[t], b_right)

    for i in range(8):
        even = infos[2 * i].astype(F32)
        oddb = infos[2 * i + 1].astype(F32)
        m0 = infos[i].astype(F32)
        m1 = infos[8 + i].astype(F32)
        e0 = jnp.broadcast_to(even[0:1], (8, 128))
        o0 = jnp.broadcast_to(oddb[0:1], (8, 128))
        dep[:, i * 128:(i + 1) * 128] = jnp.where(first, e0, o0)
        dep[:, (8 + i) * 128:(9 + i) * 128] = jnp.where(first, o0, e0)
        dep[:, (16 + i) * 128:(17 + i) * 128] = jnp.broadcast_to(m0[1:2], (8, 128))
        dep[:, (24 + i) * 128:(25 + i) * 128] = jnp.broadcast_to(m1[1:2], (8, 128))

    @pl.loop(0, N_TM)
    def _(t):
        v = infos[t].astype(F32)
        tv = jnp.broadcast_to(v[2:3] + v[3:4] + v[4:5], (8, 128))
        for g in range(32):
            cut = slice(g * 128, (g + 1) * 128)
            expo[t, :, cut] = jnp.exp(-dep[:, cut] * tv)

    @pl.loop(0, 4)
    def _(n):
        g = (group + n) % 4
        own, other = row_index(g, core), row_index(g, 1 - core)

        @pl.when(n > 0)
        def _():
            wait_recv(rowblk.at[own], r_recv.at[own], b_left)
            row_hand(n).start()

        scale_rows(own)
        wait_recv(rowblk.at[other], r_recv.at[other], b_left)
        scale_rows(other)
        pl.when(n < 3)(lambda: relay(1, n + 1))

    for k, rs in ((2, (0, 1, 2)), (3, (3, 4)), (4, (5, 6)), (5, (7,))):
        for s, r in enumerate(rs):
            load_left(s, r)

        @pl.loop(0, 4)
        def _(n):
            if k < 5:
                relay(k, n)
            product(rs, n)

    for d in range(2):
        @pl.loop(0, 8)
        def _(r):
            for h in range(2):
                wait_recv(out_ref.at[d, plus(b, offset(r)), 2 * h:2 * h + 2], p_recv.at[d, r, h], b_left)

    @pl.loop(0, N_TM)
    def _(t):
        wait_send(msg.at[t], s0_send.at[t], b_left)
        wait_send(info, i_send.at[t], b_left)

    @pl.loop(1, 8)
    def _(j):
        wait_send(blocks.at[b, a], r_send.at[j], b_left)
        wait_send(blocks.at[b, a], s1_send.at[j], b_left)

    for way in range(2):
        for k in range(3):
            @pl.loop(0, 8)
            def _(i):
                wait_send(blocks.at[b, a], s2_send.at[way, k, i], b_left)

        @pl.loop(0, 4)
        def _(i):
            wait_send(blocks.at[b, a], s2_send.at[way, 3, 4 * way + i], b_left)

        @pl.loop(0, 8)
        def _(r):
            for h in range(2):
                wait_send(ptile.at[way, r, 2 * h:2 * h + 2], p_send.at[way, r, h], b_left)


def gather_products(tp, fo, eo, fd, ed):
    hbm = pl.BlockSpec(memory_space=pltpu.HBM)
    dma = pltpu.SemaphoreType.DMA
    return pl.pallas_call(
        gather_kernel,
        out_shape=jax.ShapeDtypeStruct((2, 8, 4, 64, 128), BF16),
        in_specs=[pl.BlockSpec(memory_space=pltpu.SMEM), hbm, hbm, hbm, hbm],
        out_specs=pl.BlockSpec(memory_space=pl.ANY),
        scratch_shapes=[
            pltpu.VMEM(fo.shape, BF16), pltpu.VMEM(eo.shape, BF16),
            pltpu.VMEM(fd.shape, BF16), pltpu.VMEM(ed.shape, BF16),
            pltpu.VMEM((16, 16, 128), BF16), pltpu.VMEM((16, 16, 128), BF16),
            pltpu.VMEM((16, 128), BF16), pltpu.VMEM((16, 16, 128), BF16),
            pltpu.VMEM((8, 8, 16, KHALF), BF16),
            pltpu.VMEM((8, 16, KHALF), BF16),
            pltpu.VMEM((8, 2 * KHALF), F32),
            pltpu.VMEM((16, 8, 2 * KHALF), F32),
            pltpu.VMEM((1024, 2 * KHALF), BF16),
            pltpu.VMEM((192, 2 * KHALF), BF16),
            pltpu.VMEM((2, 8, 4, 64, 128), BF16),
            dma((4,)), dma((16,)), dma((16,)), dma((16,)), dma((16,)), dma((8,)), dma((8,)),
            dma((8,)), dma((8,)),
            dma((2, 4, 8)), dma((2, 4, 8)), dma((2, 8, 2)), dma((2, 8, 2)),
        ],
        compiler_params=pltpu.CompilerParams(
            collective_id=0, has_side_effects=True, vmem_limit_bytes=36 * 1024 * 1024),
        cost_estimate=pl.CostEstimate(flops=2 * 1024 * 4096 * 512, bytes_accessed=2 ** 22,
                                      transcendentals=2 ** 16),
        name="gather_products",
    )(tp, fo, eo, fd, ed)


def transform_kernel(w_ref, p_ref, out_ref, kw, points, result, out_sem):
    core = lax.axis_index("col") % 2
    rr = lax.broadcasted_iota(jnp.int32, (128, 16), 0)
    rc = lax.broadcasted_iota(jnp.int32, (128, 16), 1)
    up = jnp.where(rr // 8 == rc, 1.0, 0.0).astype(BF16)
    cr = lax.broadcasted_iota(jnp.int32, (16, 128), 0)
    cc = lax.broadcasted_iota(jnp.int32, (16, 128), 1)
    across = jnp.where(cc // 8 == cr, 1.0, 0.0).astype(BF16)
    r2 = lax.broadcasted_iota(jnp.int32, (128, 128), 0)
    c2 = lax.broadcasted_iota(jnp.int32, (128, 128), 1)
    keep = (r2 % 8) == (c2 % 8)
    rest = w_ref[...]
    for i in range(3):
        part = rest.astype(BF16)
        rest = rest - part.astype(F32)
        tall = jnp.dot(up, part, preferred_element_type=F32).astype(BF16)
        full = jnp.dot(tall, across, preferred_element_type=F32)
        kw[i * 128:(i + 1) * 128, :] = jnp.where(keep, full, 0.0).astype(BF16)

    stores = []
    for q in range(4):
        @pl.when(core == 0)
        def _():
            for n in range(2):
                for yp in range(8):
                    points[(2 * yp + n) * 64:(2 * yp + n + 1) * 64, :] = p_ref[n, yp, q]

        @pl.when(core == 1)
        def _():
            for n in range(2):
                v = p_ref[n, :, q].astype(F32)
                for yp in range(8):
                    piece = v[:, yp * 8:(yp + 1) * 8, :].reshape(64, 128)
                    points[(2 * yp + n) * 64:(2 * yp + n + 1) * 64, :] = piece.astype(BF16)

        for c in range(4):
            pts = points[c * 256:(c + 1) * 256, :]
            three = lax.dot_general(kw[...], pts, NT_DIMS, preferred_element_type=F32)
            total = three[256:384] + three[128:256] + three[0:128]
            result[:, q, :, c * 256:(c + 1) * 256] = total.reshape(16, 8, 256)
        store = pltpu.make_async_copy(result.at[:, q], out_ref.at[:, q], out_sem.at[q])
        store.start()
        stores.append(store)
    for store in stores:
        store.wait()


def transform(w, p):
    dma = pltpu.SemaphoreType.DMA
    return pl.pallas_call(
        transform_kernel,
        out_shape=jax.ShapeDtypeStruct((16, 4, 8, 1024), F32),
        in_specs=[pl.BlockSpec(memory_space=pltpu.VMEM)] * 2,
        out_specs=pl.BlockSpec(memory_space=pl.ANY),
        scratch_shapes=[
            pltpu.VMEM((384, 128), BF16), pltpu.VMEM((1024, 128), BF16),
            pltpu.VMEM((16, 4, 8, 1024), F32), dma((4,)),
        ],
        compiler_params=pltpu.CompilerParams(vmem_limit_bytes=36 * 1024 * 1024),
        cost_estimate=pl.CostEstimate(flops=2 ** 28, bytes_accessed=3 * 2 ** 20, transcendentals=0),
        name="transform",
    )(w, p)


def on_device(
    filled_orbitals, empty_orbitals, filled_depth, empty_depth, time_points, cosine_weights
):
    def hold(v):
        return pltpu.with_memory_space_constraint(v, pltpu.HBM)

    p = gather_products(
        time_points,
        hold(jnp.swapaxes(filled_orbitals, 1, 2).reshape(64, 128)),
        hold(jnp.swapaxes(empty_orbitals, 1, 2).reshape(192, 128)),
        hold(filled_depth),
        hold(empty_depth),
    )
    return transform(cosine_weights, p)


def solution(mesh):
    in_specs = (P("col", "row", "tm"), P("col", "row", "tm"), P("tm"), P("tm"), P("tm"), P())
    out_specs = P(None, None, ("row", "tm"), "col")
    return jax.shard_map(
        on_device, mesh=mesh, in_specs=in_specs, out_specs=out_specs, check_vma=False
    )
```

```python
import jax
import jax.numpy as jnp
from jax import lax
from jax.experimental import pallas as pl
from jax.experimental.pallas import tpu as pltpu
from jax.sharding import PartitionSpec as P

F32 = jnp.float32
BF16 = jnp.bfloat16
MESH = pl.DeviceIdType.MESH
NT_DIMS = (((1,), (1,)), ((), ()))

N_TM = 16
RING = 8
KHALF = 2048
KFILLED = 1024


def offset(i):
    return (1 - 2 * (i % 2)) * ((i + 1) // 2)


def gather_kernel(
    tp_ref, fo_ref, eo_ref, fd_ref, ed_ref, out_ref,
    fo, eo, fd, ed, msg, arrived, info, infos, blocks, rowblk, dep, expo, scaled, left, ptile,
    in_sem, s0_send, s0_recv, i_send, i_recv, r_send, r_recv, s1_send, s1_recv,
    s2_send, s2_recv, p_send, p_recv,
):
    y = lax.axis_index("row")
    col = lax.axis_index("col")
    tm = lax.axis_index("tm")
    x_lo, core = col // 2, col % 2
    x_hi, z = tm // RING, tm % RING
    flip = (1 - x_lo) * 2 + core
    a = z + core * (y - z)
    b = y + core * (z - y)
    mine = x_hi * 4 + flip

    def at(ap, bp):
        return (bp + core * (ap - bp), col, x_hi * RING + ap + core * (bp - ap))

    def plus(v, d):
        return (v + d + 2 * RING) % RING

    b_right, b_left = at(a, plus(b, 1)), at(a, plus(b, -1))

    group = x_hi * 2 + x_lo
    sibling = (y, x_lo * 2 + 1 - core, tm)

    def row_index(g, c):
        return (g // 2) * 4 + (1 - g % 2) * 2 + c

    loads = [
        pltpu.make_async_copy(src, dst, in_sem.at[i])
        for i, (src, dst) in enumerate(((fo_ref, fo), (eo_ref, eo), (fd_ref, fd), (ed_ref, ed)))
    ]
    for load in loads:
        load.start()

    barrier = pltpu.get_barrier_semaphore()

    def greet(device):
        pl.semaphore_signal(barrier, inc=1, device_id=device, device_id_type=MESH)

    def far(t):
        return (t % 2) * RING + plus(z, 4 + offset(t // 2))

    @pl.loop(0, N_TM)
    def _(t):
        greet((y, flip, far(t)))

    greet((plus(y, 1), col, tm))
    greet((plus(y, -1), col, tm))

    @pl.when(core == 1)
    def _():
        for d in (2, -2):
            greet((plus(y, d), col, tm))

    greet(sibling)

    for load in loads:
        load.wait()

    odd = tm % 2

    def arrange(f, e, axis):
        tail = lax.slice_in_dim(e, 128, 192, axis=axis)
        low = jnp.concatenate([f, tail], axis=axis)
        high = jnp.concatenate([tail, f], axis=axis)
        return jnp.where(odd == 1, high, low), lax.slice_in_dim(e, 0, 128, axis=axis)

    f0, f1 = arrange(fo[...].astype(F32), eo[...].astype(F32), 0)
    rows = jnp.concatenate([f0.T.reshape(N_TM, 8, 128), f1.T.reshape(N_TM, 8, 128)], axis=1)
    msg[...] = rows.astype(BF16)

    pl.semaphore_wait(barrier, 19 + 2 * core)

    def s0_copy(to):
        return pltpu.make_async_remote_copy(
            src_ref=msg.at[to], dst_ref=arrived.at[tm], send_sem=s0_send.at[to],
            recv_sem=s0_recv.at[tm], device_id=(y, flip, to), device_id_type=MESH)

    def info_copy(to):
        return pltpu.make_async_remote_copy(
            src_ref=info, dst_ref=infos.at[tm], send_sem=i_send.at[to],
            recv_sem=i_recv.at[tm], device_id=(y, flip, to), device_id_type=MESH)

    @pl.loop(0, N_TM)
    def _(t):
        s0_copy(far(t)).start()

    d0, d1 = arrange(fd[...].astype(F32).reshape(1, 64), ed[...].astype(F32).reshape(1, 192), 1)
    tau = jnp.full((1, 128), tp_ref[0], F32)
    t_hi = tau.astype(BF16).astype(F32)
    t_mid = (tau - t_hi).astype(BF16).astype(F32)
    t_low = tau - t_hi - t_mid
    info[...] = jnp.concatenate(
        [d0, d1, t_hi, t_mid, t_low, jnp.zeros((11, 128), F32)], axis=0).astype(BF16)

    def wait_recv(dst, sem, device):
        pltpu.make_async_remote_copy(
            src_ref=dst, dst_ref=dst, send_sem=sem, recv_sem=sem,
            device_id=device, device_id_type=MESH).wait_recv()

    def wait_send(src, sem, device):
        pltpu.make_async_remote_copy(
            src_ref=src, dst_ref=src, send_sem=sem, recv_sem=sem,
            device_id=device, device_id_type=MESH).wait_send()

    @pl.loop(0, N_TM)
    def _(t):
        wait_recv(arrived.at[t], s0_recv.at[t], b_right)

    lane = lax.broadcasted_iota(jnp.int32, (8, 128), 1)
    first = lane < 64
    for i in range(8):
        even = arrived[2 * i].astype(F32)[0:8]
        oddb = arrived[2 * i + 1].astype(F32)[0:8]
        fil = jnp.where(first, even, oddb)
        tail = jnp.where(first, oddb, even)
        m0 = arrived[i].astype(F32)[8:16]
        m1 = arrived[8 + i].astype(F32)[8:16]
        lo = jnp.concatenate([fil, m0], axis=0).astype(BF16)
        hi = jnp.concatenate([tail, m1], axis=0).astype(BF16)
        blocks[b, a, :, i * 128:(i + 1) * 128] = lo
        blocks[b, a, :, (8 + i) * 128:(9 + i) * 128] = hi
        rowblk[mine, :, i * 128:(i + 1) * 128] = lo
        rowblk[mine, :, (8 + i) * 128:(9 + i) * 128] = hi

    def s1_copy(i, d, seen):
        ref = blocks.at[b, plus(a, offset(i))]
        return pltpu.make_async_remote_copy(
            src_ref=ref, dst_ref=ref, send_sem=s1_send.at[seen], recv_sem=s1_recv.at[seen],
            device_id=at(plus(a, d), b), device_id_type=MESH)

    def s2_copy(k, i, way):
        bp = plus(b, -k if way == 0 else k)
        ref = blocks.at[bp, plus(a, offset(i))]
        return pltpu.make_async_remote_copy(
            src_ref=ref, dst_ref=ref, send_sem=s2_send.at[way, k, i],
            recv_sem=s2_recv.at[way, k, i], device_id=b_right if way == 0 else b_left,
            device_id_type=MESH)

    def row_copy(j):
        g = (group + j) % 4
        return pltpu.make_async_remote_copy(
            src_ref=blocks.at[b, a], dst_ref=rowblk.at[mine], send_sem=r_send.at[j],
            recv_sem=r_recv.at[mine], device_id=(y, (g % 2) * 2 + core, (g // 2) * RING + z),
            device_id_type=MESH)

    def row_hand(j):
        ref = rowblk.at[row_index((group + j) % 4, core)]
        return pltpu.make_async_remote_copy(
            src_ref=ref, dst_ref=ref, send_sem=r_send.at[4 + j],
            recv_sem=r_recv.at[row_index((group + j) % 4, core)], device_id=sibling,
            device_id_type=MESH)

    s2_copy(0, 0, 0).start()
    s2_copy(0, 0, 1).start()
    for d, seen in ((2, 3), (-2, 4), (1, 1), (-1, 2)):
        s1_copy(0, d, seen).start()

    @pl.loop(1, 4)
    def _(j):
        row_copy(j).start()

    row_hand(0).start()

    @pl.loop(0, N_TM)
    def _(t):
        info_copy(far(t)).start()

    def relay(k, n):
        for half in range(2):
            i = 2 * n + half

            def take(way):
                bp = plus(b, -k if way == 0 else k)
                wait_recv(blocks.at[bp, plus(a, offset(i))], s2_recv.at[way, k - 1, i], b_left)

            def hand(way):
                s2_copy(k, i, way).start()

            if k < 3:
                for way in range(2):
                    take(way)
                    hand(way)
            elif k == 3:
                take(0)
                pl.when(n < 2)(lambda: hand(0))
                take(1)
                pl.when(n >= 2)(lambda: hand(1))
            else:
                pl.when(n < 2)(lambda: take(0))
                pl.when(n >= 2)(lambda: take(1))

    def scale_rows(e):
        lo = rowblk[e].astype(F32)[0:8]
        hi = rowblk[e].astype(F32)[8:16]

        @pl.loop(0, N_TM // 2)
        def _(tp):
            at_row = pl.ds(pl.multiple_of(e * 128 + tp * 16, 16), 16)
            for part, src in ((0, lo), (1, hi)):
                cut = slice(part * KHALF, (part + 1) * KHALF)
                both = [src * expo[2 * tp + h, :, cut] for h in range(2)]
                scaled[at_row, cut] = jnp.concatenate(both, axis=0).astype(BF16)

    def load_left(slot, r):
        bp = plus(b, offset(r))

        @pl.loop(0, 4)
        def _(j):
            v = blocks[bp, pl.ds(2 * j, 2)].astype(F32)
            at_row = pl.ds(pl.multiple_of(slot * 64 + j * 16, 16), 16)
            left[at_row, 0:KHALF] = v[:, 0:8].reshape(16, KHALF).astype(BF16)
            left[at_row, KHALF:] = v[:, 8:16].reshape(16, KHALF).astype(BF16)

    def p_copy(d, r, h):
        two = pl.ds(2 * h, 2)
        return pltpu.make_async_remote_copy(
            src_ref=ptile.at[d, r, two], dst_ref=out_ref.at[x_hi, plus(b, offset(r)), two],
            send_sem=p_send.at[d, r, h], recv_sem=p_recv.at[x_hi, r, h],
            device_id=(y, flip, d * RING + z), device_id_type=MESH)

    def product(rs, n):
        m = 64 * len(rs)
        at_row = pl.ds(pl.multiple_of(n * 256, 256), 256)
        g_o = lax.dot_general(scaled[at_row, 0:KFILLED], left[0:m, 0:KFILLED], NT_DIMS,
                              preferred_element_type=F32)
        g_e = lax.dot_general(scaled[at_row, KFILLED:], left[0:m, KFILLED:], NT_DIMS,
                              preferred_element_type=F32)
        p = (-(g_o * g_e)).T.astype(BF16)
        d, q = n // 2, 2 * (n % 2)
        for s, r in enumerate(rs):
            for h in range(2):
                ptile[d, r, q + h] = p[s * 64:(s + 1) * 64, h * 128:(h + 1) * 128]

        for r in rs:
            p_copy(d, r, n % 2).start()

    for i in range(1, 8):
        wait_recv(blocks.at[b, plus(a, offset(i))], s1_recv.at[i], b_left)
        if i == 3:
            s1_copy(3, 1, 5).start()
            s1_copy(3, 2, 7).start()
        elif i == 4:
            s1_copy(4, -1, 6).start()
        s2_copy(0, i, 0).start()
        s2_copy(0, i, 1).start()
        if i == 4:
            relay(1, 0)


    @pl.loop(0, N_TM)
    def _(t):
        wait_recv(infos.at[t], i_recv.at[t], b_right)

    for i in range(8):
        even = infos[2 * i].astype(F32)
        oddb = infos[2 * i + 1].astype(F32)
        m0 = infos[i].astype(F32)
        m1 = infos[8 + i].astype(F32)
        e0 = jnp.broadcast_to(even[0:1], (8, 128))
        o0 = jnp.broadcast_to(oddb[0:1], (8, 128))
        dep[:, i * 128:(i + 1) * 128] = jnp.where(first, e0, o0)
        dep[:, (8 + i) * 128:(9 + i) * 128] = jnp.where(first, o0, e0)
        dep[:, (16 + i) * 128:(17 + i) * 128] = jnp.broadcast_to(m0[1:2], (8, 128))
        dep[:, (24 + i) * 128:(25 + i) * 128] = jnp.broadcast_to(m1[1:2], (8, 128))

    @pl.loop(0, N_TM)
    def _(t):
        v = infos[t].astype(F32)
        tv = jnp.broadcast_to(v[2:3] + v[3:4] + v[4:5], (8, 128))
        for g in range(32):
            cut = slice(g * 128, (g + 1) * 128)
            expo[t, :, cut] = jnp.exp(-dep[:, cut] * tv)

    @pl.loop(0, 4)
    def _(n):
        g = (group + n) % 4
        own, other = row_index(g, core), row_index(g, 1 - core)

        @pl.when(n > 0)
        def _():
            wait_recv(rowblk.at[own], r_recv.at[own], b_left)
            row_hand(n).start()

        scale_rows(own)
        wait_recv(rowblk.at[other], r_recv.at[other], b_left)
        scale_rows(other)
        pl.when(n < 3)(lambda: relay(1, n + 1))

    for k, rs in ((2, (0, 1, 2)), (3, (3, 4)), (4, (5, 6)), (5, (7,))):
        for s, r in enumerate(rs):
            load_left(s, r)

        @pl.loop(0, 4)
        def _(n):
            if k < 5:
                relay(k, n)
            product(rs, n)

    for d in range(2):
        @pl.loop(0, 8)
        def _(r):
            for h in range(2):
                wait_recv(out_ref.at[d, plus(b, offset(r)), 2 * h:2 * h + 2], p_recv.at[d, r, h], b_left)

    @pl.loop(0, N_TM)
    def _(t):
        wait_send(msg.at[t], s0_send.at[t], b_left)
        wait_send(info, i_send.at[t], b_left)

    @pl.loop(1, 8)
    def _(j):
        wait_send(blocks.at[b, a], r_send.at[j], b_left)
        wait_send(blocks.at[b, a], s1_send.at[j], b_left)

    for way in range(2):
        for k in range(3):
            @pl.loop(0, 8)
            def _(i):
                wait_send(blocks.at[b, a], s2_send.at[way, k, i], b_left)

        @pl.loop(0, 4)
        def _(i):
            wait_send(blocks.at[b, a], s2_send.at[way, 3, 4 * way + i], b_left)

        @pl.loop(0, 8)
        def _(r):
            for h in range(2):
                wait_send(ptile.at[way, r, 2 * h:2 * h + 2], p_send.at[way, r, h], b_left)


def gather_products(tp, fo, eo, fd, ed):
    hbm = pl.BlockSpec(memory_space=pltpu.HBM)
    dma = pltpu.SemaphoreType.DMA
    return pl.pallas_call(
        gather_kernel,
        out_shape=jax.ShapeDtypeStruct((2, 8, 4, 64, 128), BF16),
        in_specs=[pl.BlockSpec(memory_space=pltpu.SMEM), hbm, hbm, hbm, hbm],
        out_specs=pl.BlockSpec(memory_space=pl.ANY),
        scratch_shapes=[
            pltpu.VMEM(fo.shape, BF16), pltpu.VMEM(eo.shape, BF16),
            pltpu.VMEM(fd.shape, BF16), pltpu.VMEM(ed.shape, BF16),
            pltpu.VMEM((16, 16, 128), BF16), pltpu.VMEM((16, 16, 128), BF16),
            pltpu.VMEM((16, 128), BF16), pltpu.VMEM((16, 16, 128), BF16),
            pltpu.VMEM((8, 8, 16, KHALF), BF16),
            pltpu.VMEM((8, 16, KHALF), BF16),
            pltpu.VMEM((8, 2 * KHALF), F32),
            pltpu.VMEM((16, 8, 2 * KHALF), F32),
            pltpu.VMEM((1024, 2 * KHALF), BF16),
            pltpu.VMEM((192, 2 * KHALF), BF16),
            pltpu.VMEM((2, 8, 4, 64, 128), BF16),
            dma((4,)), dma((16,)), dma((16,)), dma((16,)), dma((16,)), dma((8,)), dma((8,)),
            dma((8,)), dma((8,)),
            dma((2, 4, 8)), dma((2, 4, 8)), dma((2, 8, 2)), dma((2, 8, 2)),
        ],
        compiler_params=pltpu.CompilerParams(
            collective_id=0, has_side_effects=True, vmem_limit_bytes=36 * 1024 * 1024),
        cost_estimate=pl.CostEstimate(flops=2 * 1024 * 4096 * 512, bytes_accessed=2 ** 22,
                                      transcendentals=2 ** 16),
        name="gather_products",
    )(tp, fo, eo, fd, ed)


def transform_kernel(w_ref, p_ref, out_ref, kw, points, result, out_sem):
    core = lax.axis_index("col") % 2
    rr = lax.broadcasted_iota(jnp.int32, (128, 16), 0)
    rc = lax.broadcasted_iota(jnp.int32, (128, 16), 1)
    up = jnp.where(rr // 8 == rc, 1.0, 0.0).astype(BF16)
    cr = lax.broadcasted_iota(jnp.int32, (16, 128), 0)
    cc = lax.broadcasted_iota(jnp.int32, (16, 128), 1)
    across = jnp.where(cc // 8 == cr, 1.0, 0.0).astype(BF16)
    r2 = lax.broadcasted_iota(jnp.int32, (128, 128), 0)
    c2 = lax.broadcasted_iota(jnp.int32, (128, 128), 1)
    keep = (r2 % 8) == (c2 % 8)
    rest = w_ref[...]
    for i in range(3):
        part = rest.astype(BF16)
        rest = rest - part.astype(F32)
        tall = jnp.dot(up, part, preferred_element_type=F32).astype(BF16)
        full = jnp.dot(tall, across, preferred_element_type=F32)
        kw[i * 128:(i + 1) * 128, :] = jnp.where(keep, full, 0.0).astype(BF16)

    stores = []
    for q in range(4):
        @pl.when(core == 0)
        def _():
            for n in range(2):
                for yp in range(8):
                    points[(2 * yp + n) * 64:(2 * yp + n + 1) * 64, :] = p_ref[n, yp, q]

        @pl.when(core == 1)
        def _():
            for n in range(2):
                v = p_ref[n, :, q].astype(F32)
                for yp in range(8):
                    piece = v[:, yp * 8:(yp + 1) * 8, :].reshape(64, 128)
                    points[(2 * yp + n) * 64:(2 * yp + n + 1) * 64, :] = piece.astype(BF16)

        for c in range(4):
            pts = points[c * 256:(c + 1) * 256, :]
            three = lax.dot_general(kw[...], pts, NT_DIMS, preferred_element_type=F32)
            total = three[256:384] + three[128:256] + three[0:128]
            result[:, q, :, c * 256:(c + 1) * 256] = total.reshape(16, 8, 256)
        store = pltpu.make_async_copy(result.at[:, q], out_ref.at[:, q], out_sem.at[q])
        store.start()
        stores.append(store)
    for store in stores:
        store.wait()


def transform(w, p):
    dma = pltpu.SemaphoreType.DMA
    return pl.pallas_call(
        transform_kernel,
        out_shape=jax.ShapeDtypeStruct((16, 4, 8, 1024), F32),
        in_specs=[pl.BlockSpec(memory_space=pltpu.VMEM)] * 2,
        out_specs=pl.BlockSpec(memory_space=pl.ANY),
        scratch_shapes=[
            pltpu.VMEM((384, 128), BF16), pltpu.VMEM((1024, 128), BF16),
            pltpu.VMEM((16, 4, 8, 1024), F32), dma((4,)),
        ],
        compiler_params=pltpu.CompilerParams(vmem_limit_bytes=36 * 1024 * 1024),
        cost_estimate=pl.CostEstimate(flops=2 ** 28, bytes_accessed=3 * 2 ** 20, transcendentals=0),
        name="transform",
    )(w, p)


def on_device(
    filled_orbitals, empty_orbitals, filled_depth, empty_depth, time_points, cosine_weights
):
    def hold(v):
        return pltpu.with_memory_space_constraint(v, pltpu.HBM)

    p = gather_products(
        time_points,
        hold(jnp.swapaxes(filled_orbitals, 1, 2).reshape(64, 128)),
        hold(jnp.swapaxes(empty_orbitals, 1, 2).reshape(192, 128)),
        hold(filled_depth),
        hold(empty_depth),
    )
    return transform(cosine_weights, p)


def solution(mesh):
    in_specs = (P("col", "row", "tm"), P("col", "row", "tm"), P("tm"), P("tm"), P("tm"), P())
    out_specs = P(None, None, ("row", "tm"), "col")
    return jax.shard_map(
        on_device, mesh=mesh, in_specs=in_specs, out_specs=out_specs, check_vma=False
    )
```
